256 devices in a mesh: visit: 8 (over y, core), tile: 32 (over x, z).
Axes of the slice: x: 4, y: 4, z: 8, core: 2. Of those that a mesh axis runs over, the one named last changes fastest.
Arguments:
- image: float32 [8, 1024, 4096], P('visit', 'tile'), may hold values from -6 to 6
- variance: float32 [8, 1024, 4096], P('visit', 'tile'), may hold values from 0.5 to 2
- row_mask: int32 [8, 1024], P('visit', 'tile'), may hold values 0 or 1
- row_shift: int32 [8], P('visit'), may hold values from 0 to 511
- basis_coef: float32 [8, 5], P('visit'), may hold values from -2.5 to 2.5
- vertical: float32 [5, 21], replicated, may hold values from -1.25 to 1.25
- horizontal: float32 [5, 21], replicated, may hold values from -1.25 to 1.25
- col_weight: float32 [8, 6, 4096], P('visit'), may hold values from -0.1 to 0.4
- col_offset: int32 [8, 4096], P('visit'), may hold values from 0 to 4090, as said below
- row_weight: float32 [8, 6, 1024], P('visit', None, 'tile'), may hold values from -0.1 to 0.4
Outputs:
- coadd: float32 [1024, 4096], P('tile')
- weight_sum: float32 [1024, 4096], P('tile')
The draws below stay inside these ranges and needn't reach their ends.
Inputs may be any that keep to these rules, and one draw needn't show every extreme that they name: Column c of visit v reads source columns col_offset to col_offset + 5, where col_offset lies from c - 5 to c.
All inputs are finite; a program needn't handle non-finite values. No bound on the sum of `row_mask` on one device may be relied on, other than what follows from the above.
Results may differ from the reference program's by a relative error of at most 0.0038.
Values may be sent and summed in bfloat16 or wider, within the bound.
A program may use at most 64 MiB of HBM per device.

```python
import math
import jax
import jax.numpy as jnp
from jax import lax

WIDTH = 4096
KERNEL = 21
BASES = 5
LANCZOS = 6
VISITS = 8
ROWS = 1024


def draw_col_offset(key, part):
    key = jax.random.fold_in(key, 7)
    jitter = jax.random.randint(key, (VISITS, WIDTH), -2, 3)
    base = jnp.arange(WIDTH, dtype=jnp.int32)[None, :] - 2
    return jnp.clip(base + jitter, 0, WIDTH - LANCZOS).astype(jnp.int32)


def set_ends(drawn, stream_key, least, top_value):
    place = [jax.random.randint(jax.random.fold_in(stream_key, axis), (), 0, length) for axis, length in enumerate(drawn.shape)]
    longest = drawn.shape.index(max(drawn.shape))
    beside = place[:longest] + [(place[longest] + 1) % drawn.shape[longest]] + place[longest + 1:]
    return drawn.at[tuple(place)].set(least).at[tuple(beside)].set(top_value)


def levels(stream_key, shape, cuts, least, high):
    gain = 1.0
    for axis_at, blocks in cuts:
        steps = jax.random.uniform(jax.random.fold_in(jax.random.fold_in(stream_key, 6), axis_at), (blocks,), jnp.float32, least / len(cuts), high / len(cuts))
        gain = gain * jnp.repeat(jnp.exp(steps), shape[axis_at] // blocks).reshape((-1,) + (1,) * (len(shape) - 1 - axis_at))
    return gain


def noise(own_key, dims, deviation, bound, pieces=(), held_as=jnp.bfloat16):
    array = jax.random.normal(own_key, dims, jnp.float32) * deviation
    if len(pieces) > 0:
        array = levels(own_key, dims, pieces, -0.22, 0.18) * array
    return jnp.clip(array, min=-bound, max=bound).astype(held_as)


def setup_inputs(seed: int = 0) -> dict:
    key_of = jax.random.split(jax.random.key(seed), 11)
    return {
        "image": noise(key_of[0], (VISITS, ROWS, WIDTH), 1.0, 6.0, ((0, 8), (1, 32)), jnp.float32),
        "variance": jnp.clip(jnp.exp(math.log(2.0) - 1.3862944 * jax.random.uniform(key_of[1], (VISITS, ROWS, WIDTH), jnp.float32) ** levels(key_of[1], (VISITS, ROWS, WIDTH), ((0, 8), (1, 32)), -0.2, 0.2)), 0.5, 2.0),
        "row_mask": set_ends((jax.random.randint(key_of[2], (VISITS, ROWS), 0, 8) < 7).astype(jnp.int32), jax.random.fold_in(key_of[2], 1), 0, 1),
        "row_shift": set_ends(jax.random.randint(key_of[3], (VISITS,), 0, ROWS // 2), jax.random.fold_in(key_of[3], 1), 0, (ROWS // 2) - 1).astype(jnp.int32),
        "basis_coef": noise(key_of[4], (VISITS, BASES), BASES ** -0.5, 2.5, ((0, 8),), jnp.float32),
        "vertical": noise(key_of[5], (BASES, KERNEL), KERNEL ** -0.5, 1.25, (), jnp.float32),
        "horizontal": noise(key_of[6], (BASES, KERNEL), KERNEL ** -0.5, 1.25, (), jnp.float32),
        "col_weight": jnp.clip(-0.1 + 0.5 * jax.random.uniform(key_of[7], (VISITS, LANCZOS, WIDTH), jnp.float32) ** levels(key_of[7], (VISITS, LANCZOS, WIDTH), ((0, 8),), -0.2, 0.2), -0.1, 0.4),
        "col_offset": draw_col_offset(jax.random.fold_in(key_of[10], 71), 0),
        "row_weight": jnp.clip(-0.1 + 0.5 * jax.random.uniform(key_of[9], (VISITS, LANCZOS, ROWS), jnp.float32) ** levels(key_of[9], (VISITS, LANCZOS, ROWS), ((0, 8), (2, 32)), -0.2, 0.2), -0.1, 0.4),
    }


def match_psf(padded, vertical, horizontal, weights, rows):
    kernel = vertical.shape[1]
    rim = kernel // 2
    columns = padded.shape[1]
    result = jnp.zeros((rows, columns), jnp.float32)
    for basis in range(vertical.shape[0]):
        row_pass = jnp.zeros((rows, columns), jnp.float32)
        for offset in range(kernel):
            row_pass = row_pass + vertical[basis, offset] * padded[offset:offset + rows]
        spread = jnp.pad(row_pass, ((0, 0), (rim, rim)))
        col_pass = jnp.zeros((rows, columns), jnp.float32)
        for offset in range(kernel):
            col_pass = col_pass + horizontal[basis, offset] * spread[:, offset:offset + columns]
        result = result + weights[basis] * col_pass
    return result


def warp_columns(matched, weights, offsets):
    result = jnp.zeros(matched.shape, jnp.float32)
    for offset in range(weights.shape[0]):
        result = result + weights[offset][None, :] * jnp.take(matched, offsets + offset, axis=1)
    return result


def reference(image, variance, row_mask, row_shift, basis_coef, vertical, horizontal, col_weight, col_offset, row_weight):
    rim = KERNEL // 2
    numer = jnp.zeros((ROWS, WIDTH), jnp.float32)
    denom = jnp.zeros((ROWS, WIDTH), jnp.float32)
    for visit in range(VISITS):
        padded = jnp.pad(image[visit], ((rim, rim), (0, 0)))
        matched = match_psf(padded, vertical, horizontal, basis_coef[visit], ROWS)
        colwarp = warp_columns(matched, col_weight[visit], col_offset[visit])
        ivar = row_mask[visit].astype(jnp.float32)[:, None] / variance[visit]
        moved = jnp.stack([colwarp, ivar]).astype(jnp.bfloat16)
        joined = jnp.concatenate([jnp.zeros_like(moved), moved], axis=1)
        sky = lax.dynamic_slice_in_dim(joined, (ROWS - row_shift[visit]).astype(jnp.int32), ROWS, 1)
        framed = jnp.pad(sky[0], ((3, 3), (0, 0)))
        warped = jnp.zeros((ROWS, WIDTH), jnp.float32)
        for offset in range(LANCZOS):
            warped = warped + row_weight[visit, offset][:, None] * framed[1 + offset:1 + offset + ROWS].astype(jnp.float32)
        sky_ivar = sky[1].astype(jnp.float32)
        numer = numer + sky_ivar * warped
        denom = denom + sky_ivar
    return numer / jnp.maximum(denom, 1.0), denom
```

```python
import functools

import jax
import jax.numpy as jnp
from jax import lax
from jax.experimental import pallas as pl
from jax.experimental.pallas import tpu as pltpu
from jax.sharding import PartitionSpec as P

MESH = pl.DeviceIdType.MESH
F32 = jnp.float32
BF16 = jnp.bfloat16
TAPS = 21
RIM = 10
BASES = 5
LANCZOS = 6
BLOCK = 32
SLAB = 128
PAD = 520


def split(x):
    high = x.astype(BF16)
    return high, (x - high.astype(F32)).astype(BF16)


def kernel(
    nv, nt,
    image, variance, mask, shift, coef, vert, horiz, colw, coloff, roww,
    out_c, out_w,
    x_cat, v_mat, e_hi, e_lo, o_hi, o_lo, t_main_hi, t_main_lo, t_halo_hi, t_halo_lo,
    matched, factor, rw_pad, s_iv, r_iv, s_cw, r_cw, ivf, cwf, wbi,
    nb_iv, nb_nu, c2_iv, c2_nu, total_iv, c3_iv, c3_nu, f_iv, f_nu,
    halo_send, halo_recv, send_sem, recv_sem,
):
    v, t = lax.axis_index("visit"), lax.axis_index("tile")
    depth = nt // 8
    per = nt // nv
    groups = nt // 4
    pairs = nt // 2
    rows_all = nt * BLOCK
    half = lax.rem(v, 2)
    quarter = lax.div(v, 2)
    owner = lax.div(t, per)
    to_self = (owner == v) & (lax.rem(t, 4) == quarter)

    barrier = pltpu.get_barrier_semaphore()

    def greet(v2, t2):
        pl.semaphore_signal(barrier, inc=1, device_id=(v2, t2), device_id_type=MESH)

    def greet_tile(k, c):
        greet(v, lax.rem(t + k, nt))
        return c

    def greet_visit(k, c):
        greet(lax.rem(v + k, nv), t)
        return c

    def greet_source(k, c):
        v2 = 2 * lax.rem(t, 4) + lax.rem(k, 2)
        t2 = per * v + lax.div(k, 2)

        @pl.when(jnp.logical_not((v2 == v) & (t2 == t)))
        def _():
            greet(v2, t2)

        return c

    lax.fori_loop(1, nt, greet_tile, 0)
    lax.fori_loop(1, nv, greet_visit, 0)
    lax.fori_loop(0, 2 * per, greet_source, 0)

    def cols(j, n=SLAB):
        return pl.ds(pl.multiple_of(j * n, n), n)

    def fill(j, c):
        high, low = split(image[0, :, cols(j)])
        x_cat[16:48, cols(j)] = high
        x_cat[64:96, cols(j)] = low
        x_cat[112:144, cols(j)] = high
        return c

    lax.fori_loop(0, nt, fill, 0)
    pl.semaphore_wait(barrier, (nt - 1) + (nv - 1) + groups - to_self.astype(jnp.int32))

    up = pltpu.make_async_remote_copy(
        src_ref=x_cat.at[pl.ds(32, 16)], dst_ref=x_cat.at[pl.ds(0, 16)],
        send_sem=halo_send.at[0], recv_sem=halo_recv.at[0],
        device_id=(v, lax.rem(t + 1, nt)), device_id_type=MESH)
    down = pltpu.make_async_remote_copy(
        src_ref=x_cat.at[pl.ds(16, 16)], dst_ref=x_cat.at[pl.ds(48, 16)],
        send_sem=halo_send.at[1], recv_sem=halo_recv.at[1],
        device_id=(v, lax.rem(t + nt - 1, nt)), device_id_type=MESH)
    up.start()
    down.start()

    flags = jnp.broadcast_to(mask[...].astype(F32), (BLOCK, BLOCK))
    same = lax.broadcasted_iota(jnp.int32, (BLOCK, BLOCK), 0) == lax.broadcasted_iota(jnp.int32, (BLOCK, BLOCK), 1)
    usable = jnp.sum(jnp.where(same, flags, 0.0), axis=1, keepdims=True)
    rw_pad[...] = jnp.zeros_like(rw_pad)
    for q in range(4):
        rw_pad[0:LANCZOS, BLOCK * q:BLOCK * (q + 1)] = roww[0]
    lane = lax.broadcasted_iota(jnp.int32, (8, SLAB), 1)
    placed = jnp.where(lax.div(lane, BLOCK) == lax.rem(t, 4), rw_pad[...], 0.0)
    placed_hi = placed.astype(BF16).astype(F32)
    packed = jnp.concatenate([placed_hi, placed - placed_hi], axis=0).astype(BF16)

    def weigh(j, c):
        s_iv[j, 0:BLOCK, :] = (usable / variance[0, :, cols(j)]).astype(BF16)
        s_iv[j, BLOCK:48, :] = packed
        return c

    lax.fori_loop(0, nt, weigh, 0)

    def exchange(source, target, at):
        def step(k, c):
            x = lax.rem(lax.div(t, 8) + lax.div(k, 8), depth)
            z = lax.rem(lax.rem(t, 8) + 3 * k, 8)
            t2 = x * 8 + z
            pltpu.make_async_remote_copy(
                src_ref=source.at[t2], dst_ref=target.at[t],
                send_sem=send_sem.at[at], recv_sem=recv_sem.at[at],
                device_id=(v, t2), device_id_type=MESH).start()
            return c

        lax.fori_loop(1, nt, step, 0)
        target[t] = source[t]

    def arrived(ref, at):
        pltpu.make_async_copy(ref, ref, recv_sem.at[at]).wait()

    def left(ref, at):
        pltpu.make_async_copy(ref, ref, send_sem.at[at]).wait()

    exchange(s_iv, r_iv, 0)

    r_at = lax.broadcasted_iota(jnp.int32, (BLOCK, 160), 0)
    q_at = lax.broadcasted_iota(jnp.int32, (BLOCK, 160), 1)
    q_row = jnp.where(q_at < 64, q_at - 16, jnp.where(q_at < 96, q_at - 64, q_at - 112))
    tap = q_row - r_at + RIM
    for b in range(BASES):
        value = jnp.zeros((BLOCK, 160), F32)
        for i in range(TAPS):
            value = jnp.where(tap == i, coef[0, b] * vert[b, i], value)
        high = value.astype(BF16).astype(F32)
        v_mat[BLOCK * b:BLOCK * (b + 1), :] = jnp.where(q_at < 96, high, value - high).astype(BF16)

    n_at = lax.broadcasted_iota(jnp.int32, (16, 256), 1)
    k_at = lax.broadcasted_iota(jnp.int32, (16, 256), 0)

    def band(d):
        values = [jnp.zeros((16, 256), F32) for _ in range(BASES)]
        for i in range(TAPS):
            hit = d == i
            values = [jnp.where(hit, horiz[b, i], values[b]) for b in range(BASES)]
        return [split(value) for value in values]

    def build(c, carry):
        parts = band(16 * c + k_at - n_at + RIM)
        at = pl.ds(pl.multiple_of(16 * c, 16), 16)
        for b in range(BASES):
            t_main_hi[b, at, :], t_main_lo[b, at, :] = parts[b]
            t_halo_hi[b, at, :] = jnp.zeros((16, 256), BF16)
            t_halo_lo[b, at, :] = jnp.zeros((16, 256), BF16)
        return carry

    lax.fori_loop(0, 16, build, 0)
    for start, gap in ((112, -118), (128, 138)):
        parts = band(start + k_at - n_at + gap)
        for b in range(BASES):
            t_halo_hi[b, start:start + 16, :], t_halo_lo[b, start:start + 16, :] = parts[b]

    c_at = lax.broadcasted_iota(jnp.int32, (1, 512), 1)

    def weights(g, c):
        delta = coloff[0:1, cols(g, 512)] - (c_at + 512 * g)
        sums = [jnp.zeros((1, 512), F32) for _ in range(11)]
        for gap in range(-5, 1):
            hit = delta == gap
            for k in range(LANCZOS):
                sums[gap + k + 5] = sums[gap + k + 5] + jnp.where(hit, colw[0, k:k + 1, cols(g, 512)], 0.0)
        for d in range(11):
            factor[d:d + 1, cols(g, 512)] = sums[d]
        return c

    lax.fori_loop(0, groups, weights, 0)

    for ref in (e_hi, e_lo):
        ref[:, pairs] = jnp.zeros((BASES, BLOCK, SLAB), BF16)
    for ref in (o_hi, o_lo):
        ref[:, 0] = jnp.zeros((BASES, BLOCK, SLAB), BF16)
    matched[:, 0:SLAB] = jnp.zeros((BLOCK, SLAB), F32)
    matched[:, SLAB + nt * SLAB:] = jnp.zeros((BLOCK, SLAB), F32)
    for ref in (ivf, cwf):
        ref[0:PAD, :] = jnp.zeros((PAD, SLAB), F32)
        ref[PAD + rows_all:, :] = jnp.zeros((8, SLAB), F32)

    up.wait_recv()
    down.wait_recv()

    @pl.when(t == 0)
    def _():
        x_cat[0:16, :] = jnp.zeros((16, nt * SLAB), BF16)

    @pl.when(t == nt - 1)
    def _():
        x_cat[48:64, :] = jnp.zeros((16, nt * SLAB), BF16)

    x_cat[96:112, :] = x_cat[0:16, :]
    x_cat[144:160, :] = x_cat[48:64, :]

    def vertical(j, c):
        passed = jnp.dot(v_mat[...], x_cat[:, cols(j, 256)], preferred_element_type=F32)
        for b in range(BASES):
            high, low = split(passed[BLOCK * b:BLOCK * (b + 1)])
            e_hi[b, j], o_hi[b, j + 1] = high[:, :SLAB], high[:, SLAB:]
            e_lo[b, j], o_lo[b, j + 1] = low[:, :SLAB], low[:, SLAB:]
        return c

    lax.fori_loop(0, pairs, vertical, 0)

    def horizontal(g, c):
        def side(ref, b, start):
            return ref[b, pl.ds(4 * g + start, 4)].reshape(4 * BLOCK, SLAB)

        total = jnp.zeros((4 * BLOCK, 256), F32)
        for b in range(BASES):
            main_hi = jnp.concatenate([side(e_hi, b, 0), side(o_hi, b, 1)], axis=1)
            main_lo = jnp.concatenate([side(e_lo, b, 0), side(o_lo, b, 1)], axis=1)
            halo_hi = jnp.concatenate([side(o_hi, b, 0), side(e_hi, b, 1)], axis=1)
            halo_lo = jnp.concatenate([side(o_lo, b, 0), side(e_lo, b, 1)], axis=1)
            for left_side, right_side in (
                (main_hi, t_main_hi), (main_lo, t_main_hi), (main_hi, t_main_lo),
                (halo_hi, t_halo_hi), (halo_lo, t_halo_hi), (halo_hi, t_halo_lo),
            ):
                total = total + jnp.dot(left_side, right_side[b], preferred_element_type=F32)
        for i in range(4):
            at = pl.ds(pl.multiple_of(1024 * g + 256 * i + SLAB, SLAB), 256)
            matched[:, at] = total[BLOCK * i:BLOCK * (i + 1)]
        return c

    lax.fori_loop(0, pairs // 4, horizontal, 0)

    def interpolate(g, c):
        for r in range(2):
            window = matched[16 * r:16 * (r + 1), pl.ds(pl.multiple_of(512 * g, 512), 768)]
            total = jnp.zeros((16, 512), F32)
            for d in range(-5, 6):
                moved = pltpu.roll(window, (-d) % 768, 1) if d else window
                total = total + factor[d + 5:d + 6, cols(g, 512)] * moved[:, SLAB:SLAB + 512]
            total = total.astype(BF16)
            for i in range(4):
                s_cw[4 * g + i, 16 * r:16 * (r + 1), :] = total[:, SLAB * i:SLAB * (i + 1)]
        return c

    lax.fori_loop(0, groups, interpolate, 0)
    exchange(s_cw, r_cw, 1)

    arrived(r_iv.at[pl.ds(0, nt - 1)], 0)

    def unpack(ref, target):
        def step(j, c):
            target[pl.ds(pl.multiple_of(PAD + BLOCK * j, 8), BLOCK), :] = ref[j, 0:BLOCK, :].astype(F32)
            return c

        lax.fori_loop(0, nt, step, 0)

    unpack(r_iv, ivf)
    amount = shift[0]
    pick = lax.broadcasted_iota(jnp.int32, (16, LANCZOS * SLAB), 0)
    pick = lax.rem(pick, 8) == lax.div(lax.broadcasted_iota(jnp.int32, (16, LANCZOS * SLAB), 1), SLAB)
    pick = pick.astype(F32).astype(BF16)
    row_at = lax.broadcasted_iota(jnp.int32, (SLAB, SLAB), 0)

    def spread(g, c):
        pieces = [r_iv[4 * g + q, BLOCK:48, :].astype(F32) for q in range(4)]
        joined = (pieces[0] + pieces[1] + pieces[2] + pieces[3]).astype(BF16)
        wide = lax.dot_general(joined, pick, (((0,), (0,)), ((), ())), preferred_element_type=F32)
        sky = ivf[pl.ds(SLAB * g + PAD - amount, SLAB), :]
        nb_iv[g] = sky.astype(BF16).reshape(8, 16, SLAB)
        for k in range(LANCZOS):
            inside = row_at + (SLAB * g + k - 2) < rows_all
            wbi[k, cols(g), :] = jnp.where(inside, wide[:, SLAB * k:SLAB * (k + 1)] * sky, 0.0)
        return c

    lax.fori_loop(0, groups, spread, 0)

    def scatter(source, target, at):
        def step(k, c):
            v2 = lax.rem(v + k, nv)
            pltpu.make_async_remote_copy(
                src_ref=source.at[:, v2], dst_ref=target.at[v],
                send_sem=send_sem.at[at], recv_sem=recv_sem.at[at],
                device_id=(v2, t), device_id_type=MESH).start()
            return c

        lax.fori_loop(1, nv, step, 0)
        target[v] = source[:, v]

    def deliver(source, target, at):
        rows = pl.ds(pl.multiple_of(16 * half, 16), 16)

        def step(i, c):
            t2 = 4 * i + quarter
            me = (owner == v) & (t2 == t)

            @pl.when(jnp.logical_not(me))
            def _():
                pltpu.make_async_remote_copy(
                    src_ref=source.at[i], dst_ref=target.at[t, rows],
                    send_sem=send_sem.at[at], recv_sem=recv_sem.at[at],
                    device_id=(owner, t2), device_id_type=MESH).start()

            @pl.when(me)
            def _():
                pltpu.make_async_copy(source.at[i], target.at[t, rows], recv_sem.at[at]).start()

            return c

        lax.fori_loop(0, groups, step, 0)

    def gather(target, at):
        mine = target.at[pl.ds(per * v, per)]

        def step(k, c):
            pltpu.make_async_remote_copy(
                src_ref=mine, dst_ref=mine,
                send_sem=send_sem.at[at], recv_sem=recv_sem.at[at],
                device_id=(lax.rem(v + k, nv), t), device_id_type=MESH).start()
            return c

        lax.fori_loop(1, nv, step, 0)

    def summed(ref, i):
        total = ref[0, i].astype(F32)
        for u in range(1, nv):
            total = total + ref[u, i].astype(F32)
        return total

    scatter(nb_iv, c2_iv, 2)
    arrived(c2_iv.at[pl.ds(0, nv - 1)], 2)

    def add_iv(i, c):
        total = summed(c2_iv, i)
        total_iv[i] = total
        c3_iv[i] = total.astype(BF16)
        return c

    lax.fori_loop(0, groups, add_iv, 0)
    deliver(c3_iv, f_iv, 3)
    arrived(f_iv.at[pl.ds(0, per)], 3)
    gather(f_iv, 4)

    arrived(r_cw.at[pl.ds(0, nt - 1)], 1)
    unpack(r_cw, cwf)

    def warp(g, c):
        total = jnp.zeros((SLAB, SLAB), F32)
        for k in range(LANCZOS):
            total = total + wbi[k, cols(g), :] * cwf[pl.ds(SLAB * g + PAD + k - 2 - amount, SLAB), :]
        nb_nu[g] = total.astype(BF16).reshape(8, 16, SLAB)
        return c

    lax.fori_loop(0, groups, warp, 0)
    scatter(nb_nu, c2_nu, 5)
    arrived(c2_nu.at[pl.ds(0, nv - 1)], 5)

    def add_nu(i, c):
        c3_nu[i] = (summed(c2_nu, i) / jnp.maximum(total_iv[i], 1.0)).astype(BF16)
        return c

    lax.fori_loop(0, groups, add_nu, 0)
    deliver(c3_nu, f_nu, 6)
    arrived(f_nu.at[pl.ds(0, per)], 6)
    gather(f_nu, 7)

    def emit(ref, out):
        def step(j, c):
            out[:, cols(j)] = ref[j].astype(F32)
            return c

        lax.fori_loop(0, nt, step, 0)

    arrived(f_iv.at[pl.ds(0, (nv - 1) * per)], 4)
    emit(f_iv, out_w)
    arrived(f_nu.at[pl.ds(0, (nv - 1) * per)], 7)
    emit(f_nu, out_c)

    up.wait_send()
    down.wait_send()
    left(s_iv.at[pl.ds(0, nt - 1)], 0)
    left(s_cw.at[pl.ds(0, nt - 1)], 1)
    for source, c3, final, at in ((c2_iv, c3_iv, f_iv, 2), (c2_nu, c3_nu, f_nu, 5)):
        left(source.at[pl.ds(0, nv - 1)], at)

        @pl.when(to_self)
        def _():
            left(c3.at[pl.ds(0, groups - 1)], at + 1)

        @pl.when(jnp.logical_not(to_self))
        def _():
            left(c3, at + 1)

        left(final.at[pl.ds(0, (nv - 1) * per)], at + 2)


def solution(mesh):
    nv, nt = mesh.shape["visit"], mesh.shape["tile"]
    width = nt * SLAB
    groups, pairs, per = nt // 4, nt // 2, nt // nv

    def body(*args):
        vmem = pl.BlockSpec(memory_space=pltpu.VMEM)
        smem = pl.BlockSpec(memory_space=pltpu.SMEM)

        def plane(*shape, dtype=BF16):
            return pltpu.VMEM(shape, dtype)

        return pl.pallas_call(
            functools.partial(kernel, nv, nt),
            out_shape=[jax.ShapeDtypeStruct((BLOCK, width), F32)] * 2,
            in_specs=[vmem, vmem, vmem, smem, smem, smem, smem, vmem, vmem, vmem],
            out_specs=[vmem, vmem],
            scratch_shapes=[
                plane(160, width),
                plane(160, 160),
                *[plane(BASES, pairs + 1, BLOCK, SLAB)] * 4,
                *[plane(BASES, 256, 256)] * 4,
                plane(BLOCK, width + 2 * SLAB, dtype=F32),
                plane(16, width, dtype=F32),
                plane(8, SLAB, dtype=F32),
                plane(nt, 48, SLAB), plane(nt, 48, SLAB),
                plane(nt, BLOCK, SLAB), plane(nt, BLOCK, SLAB),
                plane(PAD + nt * BLOCK + 8, SLAB, dtype=F32),
                plane(PAD + nt * BLOCK + 8, SLAB, dtype=F32),
                plane(LANCZOS, nt * BLOCK, SLAB, dtype=F32),
                *[plane(groups, 8, 16, SLAB)] * 2,
                *[plane(nv, groups, 16, SLAB)] * 2,
                plane(groups, 16, SLAB, dtype=F32),
                *[plane(groups, 16, SLAB)] * 2,
                *[plane(nt, BLOCK, SLAB)] * 2,
                pltpu.SemaphoreType.DMA((2,)),
                pltpu.SemaphoreType.DMA((2,)),
                pltpu.SemaphoreType.DMA((8,)),
                pltpu.SemaphoreType.DMA((8,)),
            ],
            compiler_params=pltpu.CompilerParams(
                collective_id=0, has_side_effects=True, vmem_limit_bytes=48 * 2**20
            ),
        )(*args)

    placed = (
        P("visit", "tile", None),
        P("visit", "tile", None),
        P("visit", "tile"),
        P("visit"),
        P("visit", None),
        P(),
        P(),
        P("visit", None, None),
        P("visit", None),
        P("visit", None, "tile"),
    )
    return jax.shard_map(
        body,
        mesh=mesh,
        in_specs=placed,
        out_specs=(P("tile", None), P("tile", None)),
        check_vma=False,
    )
```

```python
import jax
import jax.numpy as jnp
from jax import lax
from jax.experimental import pallas as pl
from jax.experimental.pallas import tpu as pltpu
from jax.sharding import PartitionSpec as P

MESH = pl.DeviceIdType.MESH
F32 = jnp.float32
BF16 = jnp.bfloat16
TAPS = 21
RIM = 10
BASES = 5
LANCZOS = 6
BLOCK = 32
SLAB = 128
PAD = 520
NV = 8
NT = 32
ROWS = NT * BLOCK
WIDTH = NT * SLAB
PAIRS = NT // 2
CHUNKS = 4
SPAN = WIDTH // CHUNKS
HALF = WIDTH // 2


def split(x):
    high = x.astype(BF16)
    return high, (x - high.astype(F32)).astype(BF16)


def cols(j, n=SLAB):
    return pl.ds(pl.multiple_of(j * n, n), n)


def far_first(k, n):
    step = lax.div(k + 1, 2)
    return lax.rem(n // 2 + step * (1 - 2 * lax.rem(k, 2)), n)


def kernel(
    image_hbm, variance_hbm, mask, shift, coef, vert, horiz, colw, coloff, roww,
    f_nu, f_iv,
    image, variance,
    x_cat, v_mat, e_hi, e_lo, o_hi, o_lo, t_main_hi, t_main_lo, t_halo_hi, t_halo_lo,
    matched, factor, rw_mine, rw_quad, rw_all, s_iv, r_iv, s_cw, r_cw, ivf, cwf, wbi,
    nb_iv, nb_nu, c2_iv, c2_nu, total_iv, c3_iv, c3_nu,
    in_sem, halo_send, halo_recv, send_sem, recv_sem,
):
    v, t = lax.axis_index("visit"), lax.axis_index("tile")
    x, z = lax.div(t, 8), lax.rem(t, 8)
    y, core = lax.div(v, 2), lax.rem(v, 2)
    quad, place = lax.div(t, 4), lax.rem(t, 4)
    side = lax.div(t, NT // 2)
    to_self = (side == core) & (lax.rem(16 - 2 * z, 4) == y)

    get_image = pltpu.make_async_copy(image_hbm.at[0], image, in_sem.at[0])
    get_variance = pltpu.make_async_copy(variance_hbm.at[0], variance, in_sem.at[1])
    get_image.start()
    get_variance.start()

    barrier = pltpu.get_barrier_semaphore()

    def greet(v2, t2):
        pl.semaphore_signal(barrier, inc=1, device_id=(v2, t2), device_id_type=MESH)

    def greet_tile(k, c):
        greet(v, lax.rem(t + k, NT))
        return c

    def greet_visit(k, c):
        greet(lax.rem(v + k, NV), t)
        return c

    lax.fori_loop(1, NT, greet_tile, 0)
    lax.fori_loop(1, NV, greet_visit, 0)

    get_image.wait()

    def fill(j, c):
        x_cat[16:48, cols(j, 512)] = image[:, cols(j, 512)].astype(BF16)
        return c

    lax.fori_loop(0, WIDTH // 512, fill, 0)
    pl.semaphore_wait(barrier, (NT - 1) + (NV - 1))

    def halo(way, g):
        from_row, to_row, t2 = ((32, 0, lax.rem(t + 1, NT)), (16, 48, lax.rem(t + NT - 1, NT)))[way]
        return pltpu.make_async_remote_copy(
            src_ref=x_cat.at[pl.ds(from_row, 16), cols(g, SPAN)], dst_ref=x_cat.at[pl.ds(to_row, 16), cols(g, SPAN)],
            send_sem=halo_send.at[way, g], recv_sem=halo_recv.at[way, g],
            device_id=(v, t2), device_id_type=MESH)

    def start_halo(g, c):
        halo(0, g).start()
        halo(1, g).start()
        return c

    lax.fori_loop(0, CHUNKS, start_halo, 0)

    def fill_low(j, c):
        high = x_cat[16:48, cols(j, 512)]
        x_cat[112:144, cols(j, 512)] = high
        x_cat[64:96, cols(j, 512)] = (image[:, cols(j, 512)] - high.astype(F32)).astype(BF16)
        return c


    def send(source, target, at, v2, t2):
        pltpu.make_async_remote_copy(
            src_ref=source, dst_ref=target, send_sem=send_sem.at[at], recv_sem=recv_sem.at[at],
            device_id=(v2, t2), device_id_type=MESH).start()

    def arrived(ref, at):
        pltpu.make_async_copy(ref, ref, recv_sem.at[at]).wait()

    def left(ref, at):
        pltpu.make_async_copy(ref, ref, send_sem.at[at]).wait()

    rw_mine[...] = jnp.zeros_like(rw_mine)
    for q in range(4):
        for k in range(LANCZOS):
            rw_mine[k:k + 1, BLOCK * q:BLOCK * (q + 1)] = roww[k]
    lane = lax.broadcasted_iota(jnp.int32, (8, SLAB), 1)
    rw_mine[...] = jnp.where(lax.div(lane, BLOCK) == place, rw_mine[...], 0.0)
    for k in range(1, 4):
        send(rw_mine, rw_quad.at[place], 6, v, 4 * quad + lax.rem(place + k, 4))
    rw_quad[place] = rw_mine[...]

    flags = jnp.broadcast_to(mask[...].astype(F32), (BLOCK, BLOCK))
    same = lax.broadcasted_iota(jnp.int32, (BLOCK, BLOCK), 0) == lax.broadcasted_iota(jnp.int32, (BLOCK, BLOCK), 1)
    usable = jnp.sum(jnp.where(same, flags, 0.0), axis=1, keepdims=True)
    get_variance.wait()

    def weigh(j, c):
        s_iv[j] = (usable / variance[:, cols(j)]).astype(BF16)
        return c

    lax.fori_loop(0, NT, weigh, 0)

    def send_iv(k, c):
        x2 = lax.rem(x + far_first(lax.rem(k, 4), 4), 4)
        z2 = lax.rem(z + far_first(lax.div(k, 4), 8), 8)
        t2 = x2 * 8 + z2
        send(s_iv.at[t2], r_iv.at[t], 0, v, t2)
        return c

    lax.fori_loop(0, NT - 1, send_iv, 0)
    r_iv[t] = s_iv[t]
    lax.fori_loop(0, WIDTH // 512, fill_low, 0)

    r_at = lax.broadcasted_iota(jnp.int32, (BLOCK, 160), 0)
    q_at = lax.broadcasted_iota(jnp.int32, (BLOCK, 160), 1)
    q_row = jnp.where(q_at < 64, q_at - 16, jnp.where(q_at < 96, q_at - 64, q_at - 112))
    tap = q_row - r_at + RIM
    for b in range(BASES):
        value = jnp.zeros((BLOCK, 160), F32)
        for i in range(TAPS):
            value = jnp.where(tap == i, coef[0, b] * vert[b, i], value)
        high = value.astype(BF16).astype(F32)
        v_mat[BLOCK * b:BLOCK * (b + 1), :] = jnp.where(q_at < 96, high, value - high).astype(BF16)

    n_at = lax.broadcasted_iota(jnp.int32, (16, 256), 1)
    k_at = lax.broadcasted_iota(jnp.int32, (16, 256), 0)

    def band(d):
        values = [jnp.zeros((16, 256), F32) for _ in range(BASES)]
        for i in range(TAPS):
            hit = d == i
            values = [jnp.where(hit, horiz[b, i], values[b]) for b in range(BASES)]
        return [split(value) for value in values]

    def build(c, carry):
        parts = band(16 * c + k_at - n_at + RIM)
        at = pl.ds(pl.multiple_of(16 * c, 16), 16)
        for b in range(BASES):
            t_main_hi[b, at, :], t_main_lo[b, at, :] = parts[b]
            t_halo_hi[b, at, :] = jnp.zeros((16, 256), BF16)
            t_halo_lo[b, at, :] = jnp.zeros((16, 256), BF16)
        return carry

    lax.fori_loop(0, 16, build, 0)
    for start, gap in ((112, -118), (128, 138)):
        parts = band(start + k_at - n_at + gap)
        for b in range(BASES):
            t_halo_hi[b, start:start + 16, :], t_halo_lo[b, start:start + 16, :] = parts[b]

    c_at = lax.broadcasted_iota(jnp.int32, (1, 512), 1)

    def weights(g, c):
        delta = coloff[0:1, cols(g, 512)] - (c_at + 512 * g)
        sums = [jnp.zeros((1, 512), F32) for _ in range(11)]
        for gap in range(-5, 1):
            hit = delta == gap
            for k in range(LANCZOS):
                sums[gap + k + 5] = sums[gap + k + 5] + jnp.where(hit, colw[k, :, cols(g, 512)], 0.0)
        for d in range(11):
            factor[d:d + 1, cols(g, 512)] = sums[d]
        return c

    lax.fori_loop(0, WIDTH // 512, weights, 0)

    for ref in (e_hi, e_lo):
        ref[:, PAIRS] = jnp.zeros((BASES, BLOCK, SLAB), BF16)
    for ref in (o_hi, o_lo):
        ref[:, 0] = jnp.zeros((BASES, BLOCK, SLAB), BF16)
    matched[:, 0:SLAB] = jnp.zeros((BLOCK, SLAB), F32)
    matched[:, SLAB + WIDTH:] = jnp.zeros((BLOCK, SLAB), F32)
    for ref in (ivf, cwf):
        ref[0:PAD, :] = jnp.zeros((PAD, SLAB), F32)
        ref[PAD + ROWS:, :] = jnp.zeros((8, SLAB), F32)

    arrived(rw_quad.at[pl.ds(0, 3)], 6)
    rw_all[quad] = rw_quad[0] + rw_quad[1] + rw_quad[2] + rw_quad[3]
    for k in range(1, 8):
        send(rw_all.at[quad], rw_all.at[quad], 7, v, 4 * lax.rem(quad + k, 8) + place)

    def vertical(g):
        for way in range(2):
            halo(way, g).wait_recv()

        @pl.when(t == 0)
        def _():
            x_cat[0:16, cols(g, SPAN)] = jnp.zeros((16, SPAN), BF16)

        @pl.when(t == NT - 1)
        def _():
            x_cat[48:64, cols(g, SPAN)] = jnp.zeros((16, SPAN), BF16)

        x_cat[96:112, cols(g, SPAN)] = x_cat[0:16, cols(g, SPAN)]
        x_cat[144:160, cols(g, SPAN)] = x_cat[48:64, cols(g, SPAN)]

        passed = jnp.dot(v_mat[...], x_cat[:, cols(g, SPAN)], preferred_element_type=F32)
        for i in range(4):
            j = 4 * g + i
            for b in range(BASES):
                high, low = split(passed[BLOCK * b:BLOCK * (b + 1), 256 * i:256 * (i + 1)])
                e_hi[b, j], o_hi[b, j + 1] = high[:, :SLAB], high[:, SLAB:]
                e_lo[b, j], o_lo[b, j + 1] = low[:, :SLAB], low[:, SLAB:]

    def horizontal(g):
        def part(ref, b, start):
            return ref[b, pl.ds(4 * g + start, 4)].reshape(4 * BLOCK, SLAB)

        total = jnp.zeros((4 * BLOCK, 256), F32)
        for b in range(BASES):
            main_hi = jnp.concatenate([part(e_hi, b, 0), part(o_hi, b, 1)], axis=1)
            main_lo = jnp.concatenate([part(e_lo, b, 0), part(o_lo, b, 1)], axis=1)
            halo_hi = jnp.concatenate([part(o_hi, b, 0), part(e_hi, b, 1)], axis=1)
            halo_lo = jnp.concatenate([part(o_lo, b, 0), part(e_lo, b, 1)], axis=1)
            for data, matrix in (
                (main_hi, t_main_hi), (main_lo, t_main_hi), (main_hi, t_main_lo),
                (halo_hi, t_halo_hi), (halo_lo, t_halo_hi), (halo_hi, t_halo_lo),
            ):
                total = total + jnp.dot(data, matrix[b], preferred_element_type=F32)
        for i in range(4):
            at = pl.ds(pl.multiple_of(SPAN * g + 256 * i + SLAB, SLAB), 256)
            matched[:, at] = total[BLOCK * i:BLOCK * (i + 1)]

    def interpolate(g):
        def step(i, c):
            j = 2 * g + i
            for r in range(2):
                window = matched[16 * r:16 * (r + 1), pl.ds(pl.multiple_of(512 * j, 512), 768)]
                total = jnp.zeros((16, 512), F32)
                for d in range(-5, 6):
                    moved = pltpu.roll(window, (-d) % 768, 1) if d else window
                    total = total + factor[d + 5:d + 6, cols(j, 512)] * moved[:, SLAB:SLAB + 512]
                total = total.astype(BF16)
                for q in range(4):
                    s_cw[4 * j + q, 16 * r:16 * (r + 1), :] = total[:, SLAB * q:SLAB * (q + 1)]
            return c

        lax.fori_loop(0, 2, step, 0)

    def send_cw(g):
        def step(k, c):
            t2 = 8 * g + lax.rem(z + far_first(k, 8), 8)

            @pl.when(t2 != t)
            def _():
                send(s_cw.at[t2], r_cw.at[t], 1, v, t2)

            return c

        lax.fori_loop(0, 8, step, 0)

    def chunk(s, c):
        @pl.when(s < CHUNKS)
        def _():
            vertical(s)

        @pl.when((s >= 1) & (s < CHUNKS + 1))
        def _():
            horizontal(s - 1)

        @pl.when(s >= 2)
        def _():
            interpolate(s - 2)
            send_cw(s - 2)

        return c

    lax.fori_loop(0, CHUNKS + 2, chunk, 0)
    r_cw[t] = s_cw[t]

    def unpack(ref, target):
        def step(j, c):
            target[pl.ds(pl.multiple_of(PAD + BLOCK * j, 8), BLOCK), :] = ref[j].astype(F32)
            return c

        lax.fori_loop(0, NT, step, 0)

    def share(ref, g, plane):
        plane = plane.astype(BF16)
        for q in range(4):
            z2 = 4 * lax.rem(g, 2) + q
            u2 = 2 * lax.rem(lax.div(g, 2) + 24 - z2 - x - z, 4)
            ref[z2, pl.ds(u2, 2)] = plane[BLOCK * q:BLOCK * (q + 1)].reshape(2, 16, SLAB)

    arrived(r_iv.at[pl.ds(0, NT - 1)], 0)
    arrived(rw_all.at[pl.ds(0, 7)], 7)
    unpack(r_iv, ivf)
    amount = shift[0]
    pick = lax.broadcasted_iota(jnp.int32, (16, LANCZOS * SLAB), 0)
    pick = lax.rem(pick, 8) == lax.div(lax.broadcasted_iota(jnp.int32, (16, LANCZOS * SLAB), 1), SLAB)
    pick = pick.astype(F32).astype(BF16)
    row_at = lax.broadcasted_iota(jnp.int32, (SLAB, SLAB), 0)

    def spread(g, c):
        whole = rw_all[g]
        high = whole.astype(BF16).astype(F32)
        joined = jnp.concatenate([high, whole - high], axis=0).astype(BF16)
        wide = lax.dot_general(joined, pick, (((0,), (0,)), ((), ())), preferred_element_type=F32)
        sky = ivf[pl.ds(SLAB * g + PAD - amount, SLAB), :]
        share(nb_iv, g, sky)
        for k in range(LANCZOS):
            inside = row_at + (SLAB * g + k - 2) < ROWS
            wbi[k, cols(g), :] = jnp.where(inside, wide[:, SLAB * k:SLAB * (k + 1)] * sky, 0.0)
        return c

    lax.fori_loop(0, 8, spread, 0)

    def scatter(source, target, at):
        def step(k, c):
            v2 = lax.rem(v + far_first(k, NV), NV)
            send(source.at[:, v2], target.at[v], at, v2, t)
            return c

        lax.fori_loop(0, NV - 1, step, 0)
        target[v] = source[:, v]

    def deliver(source, target, at):
        rows, columns = pl.ds(pl.multiple_of(16 * core, 16), 16), cols(t)

        def step(k, c):
            z2 = lax.rem(z + far_first(k, 8), 8)
            t2 = 8 * lax.rem(y + z2 + x + z, 4) + z2
            for gap in (2, 1, 3):
                send(source.at[z2], target.at[rows, columns], at, 2 * lax.rem(y + gap, 4) + side, t2)
            me = (side == core) & (t2 == t)

            @pl.when(jnp.logical_not(me))
            def _():
                send(source.at[z2], target.at[rows, columns], at, 2 * y + side, t2)

            @pl.when(me)
            def _():
                pltpu.make_async_copy(source.at[z2], target.at[rows, columns], recv_sem.at[at]).start()

            return c

        lax.fori_loop(0, 8, step, 0)

    def swap(target, at):
        mine = target.at[:, cols(core, HALF)]
        send(mine, mine, at, v + 1 - 2 * core, t)

    def summed(ref, i):
        total = ref[0, i].astype(F32)
        for u in range(1, NV):
            total = total + ref[u, i].astype(F32)
        return total

    scatter(nb_iv, c2_iv, 2)

    arrived(r_cw.at[pl.ds(0, NT - 1)], 1)
    unpack(r_cw, cwf)

    def warp(g, c):
        total = jnp.zeros((SLAB, SLAB), F32)
        for k in range(LANCZOS):
            total = total + wbi[k, cols(g), :] * cwf[pl.ds(SLAB * g + PAD + k - 2 - amount, SLAB), :]
        share(nb_nu, g, total)
        return c

    lax.fori_loop(0, 8, warp, 0)
    scatter(nb_nu, c2_nu, 3)

    arrived(c2_iv.at[pl.ds(0, NV - 1)], 2)

    def add_iv(i, c):
        total = summed(c2_iv, i)
        total_iv[i] = total
        c3_iv[i] = total.astype(BF16)
        return c

    lax.fori_loop(0, 8, add_iv, 0)
    deliver(c3_iv, f_iv, 4)

    arrived(c2_nu.at[pl.ds(0, NV - 1)], 3)

    def add_nu(i, c):
        c3_nu[i] = (summed(c2_nu, i) / jnp.maximum(total_iv[i], 1.0)).astype(BF16)
        return c

    lax.fori_loop(0, 8, add_nu, 0)
    deliver(c3_nu, f_nu, 5)

    arrived(f_iv.at[:, pl.ds(0, HALF)], 4)
    swap(f_iv, 8)
    arrived(f_nu.at[:, pl.ds(0, HALF)], 5)
    swap(f_nu, 9)

    def halo_left(g, c):
        halo(0, g).wait_send()
        halo(1, g).wait_send()
        return c

    lax.fori_loop(0, CHUNKS, halo_left, 0)
    left(rw_quad.at[pl.ds(0, 3)], 6)
    left(rw_all.at[pl.ds(0, 7)], 7)
    left(s_iv.at[pl.ds(0, NT - 1)], 0)
    left(s_cw.at[pl.ds(0, NT - 1)], 1)
    left(c2_iv.at[pl.ds(0, NV - 1)], 2)
    left(c2_nu.at[pl.ds(0, NV - 1)], 3)
    for c3, at in ((c3_iv, 4), (c3_nu, 5)):
        @pl.when(to_self)
        def _():
            left(c3.at[pl.ds(0, NT - 1)], at)

        @pl.when(jnp.logical_not(to_self))
        def _():
            left(c3, at)

    for target, at in ((f_iv, 8), (f_nu, 9)):
        left(target.at[:, pl.ds(0, HALF)], at)
        arrived(target.at[:, pl.ds(0, HALF)], at)


def solution(mesh):
    def body(image, variance, mask, shift, coef, vert, horiz, colw, coloff, roww):
        vmem = pl.BlockSpec(memory_space=pltpu.VMEM)
        smem = pl.BlockSpec(memory_space=pltpu.SMEM)
        hbm = pl.BlockSpec(memory_space=pltpu.HBM)

        def plane(*shape, dtype=BF16):
            return pltpu.VMEM(shape, dtype)

        coadd, weight_sum = pl.pallas_call(
            kernel,
            out_shape=[jax.ShapeDtypeStruct((BLOCK, WIDTH), BF16)] * 2,
            in_specs=[hbm, hbm, vmem, smem, smem, smem, smem, vmem, vmem, vmem],
            out_specs=[vmem, vmem],
            scratch_shapes=[
                *[plane(BLOCK, WIDTH, dtype=F32)] * 2,
                plane(160, WIDTH),
                plane(160, 160),
                *[plane(BASES, PAIRS + 1, BLOCK, SLAB)] * 4,
                *[plane(BASES, 256, 256)] * 4,
                plane(BLOCK, WIDTH + 2 * SLAB, dtype=F32),
                plane(16, WIDTH, dtype=F32),
                plane(8, SLAB, dtype=F32),
                plane(4, 8, SLAB, dtype=F32),
                plane(8, 8, SLAB, dtype=F32),
                *[plane(NT, BLOCK, SLAB)] * 4,
                *[plane(PAD + ROWS + 8, SLAB, dtype=F32)] * 2,
                plane(LANCZOS, ROWS, SLAB, dtype=F32),
                *[plane(8, NV, 16, SLAB)] * 2,
                *[plane(NV, 8, 16, SLAB)] * 2,
                plane(8, 16, SLAB, dtype=F32),
                *[plane(NT, 16, SLAB)] * 2,
                pltpu.SemaphoreType.DMA((2,)),
                pltpu.SemaphoreType.DMA((2, CHUNKS)),
                pltpu.SemaphoreType.DMA((2, CHUNKS)),
                pltpu.SemaphoreType.DMA((10,)),
                pltpu.SemaphoreType.DMA((10,)),
            ],
            compiler_params=pltpu.CompilerParams(
                collective_id=0, has_side_effects=True, vmem_limit_bytes=60 * 2**20
            ),
        )(image, variance, mask, shift, coef, vert, horiz,
          jnp.transpose(colw, (1, 0, 2)), coloff, jnp.transpose(roww, (1, 0, 2)))
        return coadd.astype(F32), weight_sum.astype(F32)

    placed = (
        P("visit", "tile", None),
        P("visit", "tile", None),
        P("visit", "tile"),
        P("visit"),
        P("visit", None),
        P(),
        P(),
        P("visit", None, None),
        P("visit", None),
        P("visit", None, "tile"),
    )
    return jax.shard_map(
        body,
        mesh=mesh,
        in_specs=placed,
        out_specs=(P("tile", None), P("tile", None)),
        check_vma=False,
    )
```

```python
import jax
import jax.numpy as jnp
from jax import lax
from jax.experimental import pallas as pl
from jax.experimental.pallas import tpu as pltpu
from jax.sharding import PartitionSpec as P

MESH = pl.DeviceIdType.MESH
F32 = jnp.float32
BF16 = jnp.bfloat16
TAPS = 21
RIM = 10
BASES = 5
LANCZOS = 6
BLOCK = 32
SLAB = 128
PAD = 520
NV = 8
NT = 32
ROWS = NT * BLOCK
WIDTH = NT * SLAB
PAIRS = NT // 2
CHUNKS = 4
SPAN = WIDTH // CHUNKS
HALF = WIDTH // 2


def split(x):
    high = x.astype(BF16)
    return high, (x - high.astype(F32)).astype(BF16)


def cols(j, n=SLAB):
    return pl.ds(pl.multiple_of(j * n, n), n)


def far_first(n):
    return sorted(range(n), key=lambda gap: -min(gap, n - gap))


def kernel(
    image_hbm, variance_hbm, mask_hbm, shift, coef_hbm, vert_hbm, horiz_hbm, colw_hbm, coloff_hbm, roww_hbm,
    final,
    mask, coef, vert, horiz, colw, coloff, roww,
    image, variance,
    x_cat, v_mat, e_hi, e_lo, o_hi, o_lo, t_main_hi, t_main_lo, t_halo_hi, t_halo_lo,
    matched, factor, rw_mine, rw_quad, rw_all, s_iv, r_iv, s_cw, r_cw, ivf, cwf, wbi,
    nb_iv, nb_nu, c2_iv, c2_nu, total_iv, c3_iv, c3_nu,
    in_sem, halo_send, halo_recv, send_sem, recv_sem,
):
    v, t = lax.axis_index("visit"), lax.axis_index("tile")
    f_nu, f_iv = final.at[pl.ds(0, BLOCK)], final.at[pl.ds(BLOCK, BLOCK)]
    x, z = lax.div(t, 8), lax.rem(t, 8)
    y, core = lax.div(v, 2), lax.rem(v, 2)
    quad, place = lax.div(t, 4), lax.rem(t, 4)
    side = lax.div(t, NT // 2)
    to_self = (side == core) & (lax.rem(16 - 2 * z, 4) == y)

    get_image = pltpu.make_async_copy(image_hbm.at[0], image, in_sem.at[0])
    get_variance = pltpu.make_async_copy(variance_hbm.at[0], variance, in_sem.at[1])
    get_image.start()
    small = [
        pltpu.make_async_copy(source, target, in_sem.at[i + 2])
        for i, (source, target) in enumerate((
            (mask_hbm, mask), (roww_hbm, roww), (coef_hbm, coef), (vert_hbm, vert),
            (horiz_hbm, horiz), (colw_hbm, colw), (coloff_hbm, coloff)))
    ]
    for get in small:
        get.start()
    get_variance.start()

    barrier = pltpu.get_barrier_semaphore()

    def greet(v2, t2):
        pl.semaphore_signal(barrier, inc=1, device_id=(v2, t2), device_id_type=MESH)

    x_at = [8 * lax.rem(x + gap, 4) for gap in range(4)]
    z_at = [lax.rem(z + gap, 8) for gap in range(8)]
    y_at = [2 * lax.rem(y + gap, 4) for gap in range(4)]
    tiles = sorted(((dx, dz) for dx in range(4) for dz in range(8)), key=lambda gap: -min(gap[0], 4 - gap[0]) - min(gap[1], 8 - gap[1]))
    for dx, dz in tiles[:-1]:
        greet(v, x_at[dx] + z_at[dz])
    other = 1 - core
    for gap in (2, 1, 3):
        greet(y_at[gap] + core, t)
        greet(y_at[gap] + other, t)
    greet(y_at[0] + other, t)

    get_image.wait()

    def fill(j, c):
        x_cat[16:48, cols(j, 512)] = image[:, cols(j, 512)].astype(BF16)
        return c

    lax.fori_loop(0, WIDTH // 512, fill, 0)
    pl.semaphore_wait(barrier, (NT - 1) + (NV - 1))

    def halo(way, g):
        from_row, to_row, t2 = ((32, 0, lax.rem(t + 1, NT)), (16, 48, lax.rem(t + NT - 1, NT)))[way]
        return pltpu.make_async_remote_copy(
            src_ref=x_cat.at[pl.ds(from_row, 16), cols(g, SPAN)], dst_ref=x_cat.at[pl.ds(to_row, 16), cols(g, SPAN)],
            send_sem=halo_send.at[way, g], recv_sem=halo_recv.at[way, g],
            device_id=(v, t2), device_id_type=MESH)

    def start_halo(g, c):
        halo(0, g).start()
        halo(1, g).start()
        return c

    lax.fori_loop(0, CHUNKS, start_halo, 0)

    def fill_low(j, c):
        high = x_cat[16:48, cols(j, 512)]
        x_cat[112:144, cols(j, 512)] = high
        x_cat[64:96, cols(j, 512)] = (image[:, cols(j, 512)] - high.astype(F32)).astype(BF16)
        return c


    def send(source, target, at, v2, t2):
        pltpu.make_async_remote_copy(
            src_ref=source, dst_ref=target, send_sem=send_sem.at[at], recv_sem=recv_sem.at[at],
            device_id=(v2, t2), device_id_type=MESH).start()

    def arrived(ref, at):
        pltpu.make_async_copy(ref, ref, recv_sem.at[at]).wait()

    def left(ref, at):
        pltpu.make_async_copy(ref, ref, send_sem.at[at]).wait()

    for get in small:
        get.wait()
    rw_mine[...] = jnp.zeros_like(rw_mine)
    for q in range(4):
        for k in range(LANCZOS):
            rw_mine[k:k + 1, BLOCK * q:BLOCK * (q + 1)] = roww[k]
    lane = lax.broadcasted_iota(jnp.int32, (8, SLAB), 1)
    rw_mine[...] = jnp.where(lax.div(lane, BLOCK) == place, rw_mine[...], 0.0)
    for k in range(1, 4):
        send(rw_mine, rw_quad.at[place], 6, v, 4 * quad + lax.rem(place + k, 4))
    rw_quad[place] = rw_mine[...]

    flags = jnp.broadcast_to(mask[...].astype(F32), (BLOCK, BLOCK))
    same = lax.broadcasted_iota(jnp.int32, (BLOCK, BLOCK), 0) == lax.broadcasted_iota(jnp.int32, (BLOCK, BLOCK), 1)
    usable = jnp.sum(jnp.where(same, flags, 0.0), axis=1, keepdims=True)
    get_variance.wait()

    def weigh(j, c):
        s_iv[j] = (usable / variance[:, cols(j)]).astype(BF16)
        return c

    lax.fori_loop(0, NT, weigh, 0)

    for dx, dz in tiles[:-1]:
        t2 = x_at[dx] + z_at[dz]
        send(s_iv.at[t2], r_iv.at[t], 0, v, t2)
    r_iv[t] = s_iv[t]
    lax.fori_loop(0, WIDTH // 512, fill_low, 0)

    r_at = lax.broadcasted_iota(jnp.int32, (BLOCK, 160), 0)
    q_at = lax.broadcasted_iota(jnp.int32, (BLOCK, 160), 1)
    q_row = jnp.where(q_at < 64, q_at - 16, jnp.where(q_at < 96, q_at - 64, q_at - 112))
    tap = q_row - r_at + RIM
    for b in range(BASES):
        value = jnp.zeros((BLOCK, 160), F32)
        for i in range(TAPS):
            value = jnp.where(tap == i, coef[0, b] * vert[b, i], value)
        high = value.astype(BF16).astype(F32)
        v_mat[BLOCK * b:BLOCK * (b + 1), :] = jnp.where(q_at < 96, high, value - high).astype(BF16)

    n_at = lax.broadcasted_iota(jnp.int32, (16, 256), 1)
    k_at = lax.broadcasted_iota(jnp.int32, (16, 256), 0)

    def band(d):
        values = [jnp.zeros((16, 256), F32) for _ in range(BASES)]
        for i in range(TAPS):
            hit = d == i
            values = [jnp.where(hit, horiz[b, i], values[b]) for b in range(BASES)]
        return [split(value) for value in values]

    def build(c, carry):
        parts = band(16 * c + k_at - n_at + RIM)
        at = pl.ds(pl.multiple_of(16 * c, 16), 16)
        for b in range(BASES):
            t_main_hi[b, at, :], t_main_lo[b, at, :] = parts[b]
            t_halo_hi[b, at, :] = jnp.zeros((16, 256), BF16)
            t_halo_lo[b, at, :] = jnp.zeros((16, 256), BF16)
        return carry

    lax.fori_loop(0, 16, build, 0)
    for start, gap in ((112, -118), (128, 138)):
        parts = band(start + k_at - n_at + gap)
        for b in range(BASES):
            t_halo_hi[b, start:start + 16, :], t_halo_lo[b, start:start + 16, :] = parts[b]

    c_at = lax.broadcasted_iota(jnp.int32, (1, 512), 1)

    def weights(g, c):
        delta = coloff[0:1, cols(g, 512)] - (c_at + 512 * g)
        sums = [jnp.zeros((1, 512), F32) for _ in range(11)]
        for gap in range(-5, 1):
            hit = delta == gap
            for k in range(LANCZOS):
                sums[gap + k + 5] = sums[gap + k + 5] + jnp.where(hit, colw[k, :, cols(g, 512)], 0.0)
        for d in range(11):
            factor[d:d + 1, cols(g, 512)] = sums[d]
        return c

    lax.fori_loop(0, WIDTH // 512, weights, 0)

    for ref in (e_hi, e_lo):
        ref[:, PAIRS] = jnp.zeros((BASES, BLOCK, SLAB), BF16)
    for ref in (o_hi, o_lo):
        ref[:, 0] = jnp.zeros((BASES, BLOCK, SLAB), BF16)
    matched[:, 0:SLAB] = jnp.zeros((BLOCK, SLAB), F32)
    matched[:, SLAB + WIDTH:] = jnp.zeros((BLOCK, SLAB), F32)
    for ref in (ivf, cwf):
        ref[0:PAD, :] = jnp.zeros((PAD, SLAB), F32)
        ref[PAD + ROWS:, :] = jnp.zeros((8, SLAB), F32)

    arrived(rw_quad.at[pl.ds(0, 3)], 6)
    rw_all[quad] = rw_quad[0] + rw_quad[1] + rw_quad[2] + rw_quad[3]
    for k in range(1, 8):
        send(rw_all.at[quad], rw_all.at[quad], 7, v, 4 * lax.rem(quad + k, 8) + place)

    def vertical(g):
        for way in range(2):
            halo(way, g).wait_recv()

        @pl.when(t == 0)
        def _():
            x_cat[0:16, cols(g, SPAN)] = jnp.zeros((16, SPAN), BF16)

        @pl.when(t == NT - 1)
        def _():
            x_cat[48:64, cols(g, SPAN)] = jnp.zeros((16, SPAN), BF16)

        x_cat[96:112, cols(g, SPAN)] = x_cat[0:16, cols(g, SPAN)]
        x_cat[144:160, cols(g, SPAN)] = x_cat[48:64, cols(g, SPAN)]

        passed = jnp.dot(v_mat[...], x_cat[:, cols(g, SPAN)], preferred_element_type=F32)
        for i in range(4):
            j = 4 * g + i
            for b in range(BASES):
                high, low = split(passed[BLOCK * b:BLOCK * (b + 1), 256 * i:256 * (i + 1)])
                e_hi[b, j], o_hi[b, j + 1] = high[:, :SLAB], high[:, SLAB:]
                e_lo[b, j], o_lo[b, j + 1] = low[:, :SLAB], low[:, SLAB:]

    def horizontal(g):
        def part(ref, b, start):
            return ref[b, pl.ds(4 * g + start, 4)].reshape(4 * BLOCK, SLAB)

        total = jnp.zeros((4 * BLOCK, 256), F32)
        for b in range(BASES):
            main_hi = jnp.concatenate([part(e_hi, b, 0), part(o_hi, b, 1)], axis=1)
            main_lo = jnp.concatenate([part(e_lo, b, 0), part(o_lo, b, 1)], axis=1)
            halo_hi = jnp.concatenate([part(o_hi, b, 0), part(e_hi, b, 1)], axis=1)
            halo_lo = jnp.concatenate([part(o_lo, b, 0), part(e_lo, b, 1)], axis=1)
            for data, matrix in (
                (main_hi, t_main_hi), (main_lo, t_main_hi), (main_hi, t_main_lo),
                (halo_hi, t_halo_hi), (halo_lo, t_halo_hi), (halo_hi, t_halo_lo),
            ):
                total = total + jnp.dot(data, matrix[b], preferred_element_type=F32)
        for i in range(4):
            at = pl.ds(pl.multiple_of(SPAN * g + 256 * i + SLAB, SLAB), 256)
            matched[:, at] = total[BLOCK * i:BLOCK * (i + 1)]

    def interpolate(g):
        def step(i, c):
            j = 2 * g + i
            for r in range(2):
                window = matched[16 * r:16 * (r + 1), pl.ds(pl.multiple_of(512 * j, 512), 768)]
                total = jnp.zeros((16, 512), F32)
                for d in range(-5, 6):
                    moved = pltpu.roll(window, (-d) % 768, 1) if d else window
                    total = total + factor[d + 5:d + 6, cols(j, 512)] * moved[:, SLAB:SLAB + 512]
                total = total.astype(BF16)
                for q in range(4):
                    s_cw[4 * j + q, 16 * r:16 * (r + 1), :] = total[:, SLAB * q:SLAB * (q + 1)]
            return c

        lax.fori_loop(0, 2, step, 0)

    def send_cw(g):
        for dz in far_first(8)[:-1]:
            t2 = 8 * g + z_at[dz]
            send(s_cw.at[t2], r_cw.at[t], 1, v, t2)

        @pl.when(g != x)
        def _():
            send(s_cw.at[8 * g + z], r_cw.at[t], 1, v, 8 * g + z)

    def chunk(s, c):
        @pl.when(s < CHUNKS)
        def _():
            vertical(s)

        @pl.when((s >= 1) & (s < CHUNKS + 1))
        def _():
            horizontal(s - 1)

        @pl.when(s >= 2)
        def _():
            interpolate(s - 2)
            send_cw(s - 2)

        return c

    lax.fori_loop(0, CHUNKS + 2, chunk, 0)
    r_cw[t] = s_cw[t]

    def unpack(ref, target):
        def step(j, c):
            target[pl.ds(pl.multiple_of(PAD + BLOCK * j, 8), BLOCK), :] = ref[j].astype(F32)
            return c

        lax.fori_loop(0, NT, step, 0)

    def share(ref, g, plane):
        plane = plane.astype(BF16)
        for q in range(4):
            z2 = 4 * lax.rem(g, 2) + q
            u2 = 2 * lax.rem(lax.div(g, 2) + 24 - z2 - x - z, 4)
            ref[z2, pl.ds(u2, 2)] = plane[BLOCK * q:BLOCK * (q + 1)].reshape(2, 16, SLAB)

    arrived(r_iv.at[pl.ds(0, NT - 1)], 0)
    arrived(rw_all.at[pl.ds(0, 7)], 7)
    unpack(r_iv, ivf)
    amount = shift[0]
    pick = lax.broadcasted_iota(jnp.int32, (16, LANCZOS * SLAB), 0)
    pick = lax.rem(pick, 8) == lax.div(lax.broadcasted_iota(jnp.int32, (16, LANCZOS * SLAB), 1), SLAB)
    pick = pick.astype(F32).astype(BF16)
    row_at = lax.broadcasted_iota(jnp.int32, (SLAB, SLAB), 0)

    def spread(g, c):
        whole = rw_all[g]
        high = whole.astype(BF16).astype(F32)
        joined = jnp.concatenate([high, whole - high], axis=0).astype(BF16)
        wide = lax.dot_general(joined, pick, (((0,), (0,)), ((), ())), preferred_element_type=F32)
        sky = ivf[pl.ds(SLAB * g + PAD - amount, SLAB), :]
        share(nb_iv, g, sky)
        for k in range(LANCZOS):
            inside = row_at + (SLAB * g + k - 2) < ROWS
            wbi[k, cols(g), :] = jnp.where(inside, wide[:, SLAB * k:SLAB * (k + 1)] * sky, 0.0)
        return c

    lax.fori_loop(0, 8, spread, 0)

    def scatter(source, target, at):
        for gap in (2, 1, 3, 0):
            for seat in (core, other) if gap else (other,):
                v2 = y_at[gap] + seat
                send(source.at[:, v2], target.at[v], at, v2, t)
        target[v] = source[:, v]

    def deliver(source, target, at):
        rows, columns = pl.ds(pl.multiple_of(16 * core, 16), 16), cols(t)

        for dz in far_first(8):
            z2 = z_at[dz]
            t2 = 8 * lax.rem(y + z2 + x + z, 4) + z2
            for gap in (2, 1, 3):
                send(source.at[z2], target.at[rows, columns], at, y_at[gap] + side, t2)
            if dz:
                send(source.at[z2], target.at[rows, columns], at, y_at[0] + side, t2)
        t2 = 8 * lax.rem(y + 2 * z + x, 4) + z
        me = (side == core) & (t2 == t)

        @pl.when(jnp.logical_not(me))
        def _():
            send(source.at[z], target.at[rows, columns], at, y_at[0] + side, t2)

        @pl.when(me)
        def _():
            pltpu.make_async_copy(source.at[z], target.at[rows, columns], recv_sem.at[at]).start()

    def swap(target, at):
        mine = target.at[:, cols(core, HALF)]
        send(mine, mine, at, v + 1 - 2 * core, t)

    def summed(ref, i):
        total = ref[0, i].astype(F32)
        for u in range(1, NV):
            total = total + ref[u, i].astype(F32)
        return total

    scatter(nb_iv, c2_iv, 2)

    arrived(r_cw.at[pl.ds(0, NT - 1)], 1)
    unpack(r_cw, cwf)

    def warp(g, c):
        total = jnp.zeros((SLAB, SLAB), F32)
        for k in range(LANCZOS):
            total = total + wbi[k, cols(g), :] * cwf[pl.ds(SLAB * g + PAD + k - 2 - amount, SLAB), :]
        share(nb_nu, g, total)
        return c

    lax.fori_loop(0, 8, warp, 0)
    scatter(nb_nu, c2_nu, 3)

    arrived(c2_iv.at[pl.ds(0, NV - 1)], 2)

    def add_iv(i, c):
        total = summed(c2_iv, i)
        total_iv[i] = total
        c3_iv[i] = total.astype(BF16)
        return c

    lax.fori_loop(0, 8, add_iv, 0)
    deliver(c3_iv, f_iv, 4)

    arrived(c2_nu.at[pl.ds(0, NV - 1)], 3)

    def add_nu(i, c):
        c3_nu[i] = (summed(c2_nu, i) / jnp.maximum(total_iv[i], 1.0)).astype(BF16)
        return c

    lax.fori_loop(0, 8, add_nu, 0)
    deliver(c3_nu, f_nu, 5)

    arrived(f_iv.at[:, pl.ds(0, HALF)], 4)
    swap(f_iv, 8)
    arrived(f_nu.at[:, pl.ds(0, HALF)], 5)
    swap(f_nu, 9)

    def halo_left(g, c):
        halo(0, g).wait_send()
        halo(1, g).wait_send()
        return c

    lax.fori_loop(0, CHUNKS, halo_left, 0)
    left(rw_quad.at[pl.ds(0, 3)], 6)
    left(rw_all.at[pl.ds(0, 7)], 7)
    left(s_iv.at[pl.ds(0, NT - 1)], 0)
    left(s_cw.at[pl.ds(0, NT - 1)], 1)
    left(c2_iv.at[pl.ds(0, NV - 1)], 2)
    left(c2_nu.at[pl.ds(0, NV - 1)], 3)
    for c3, at in ((c3_iv, 4), (c3_nu, 5)):
        @pl.when(to_self)
        def _():
            left(c3.at[pl.ds(0, NT - 1)], at)

        @pl.when(jnp.logical_not(to_self))
        def _():
            left(c3, at)

    for target, at in ((f_iv, 8), (f_nu, 9)):
        left(target.at[:, pl.ds(0, HALF)], at)
        arrived(target.at[:, pl.ds(0, HALF)], at)


def solution(mesh):
    def body(image, variance, mask, shift, coef, vert, horiz, colw, coloff, roww):
        vmem = pl.BlockSpec(memory_space=pltpu.VMEM)
        smem = pl.BlockSpec(memory_space=pltpu.SMEM)
        hbm = pl.BlockSpec(memory_space=pltpu.HBM)

        def plane(*shape, dtype=BF16):
            return pltpu.VMEM(shape, dtype)

        both = pl.pallas_call(
            kernel,
            out_shape=jax.ShapeDtypeStruct((2 * BLOCK, WIDTH), BF16),
            in_specs=[hbm, hbm, hbm, smem, *[hbm] * 6],
            out_specs=vmem,
            scratch_shapes=[
                plane(1, BLOCK, dtype=jnp.int32),
                pltpu.SMEM((1, BASES), F32),
                pltpu.SMEM((BASES, TAPS), F32),
                pltpu.SMEM((BASES, TAPS), F32),
                plane(LANCZOS, 1, WIDTH, dtype=F32),
                plane(1, WIDTH, dtype=jnp.int32),
                plane(LANCZOS, 1, BLOCK, dtype=F32),
                *[plane(BLOCK, WIDTH, dtype=F32)] * 2,
                plane(160, WIDTH),
                plane(160, 160),
                *[plane(BASES, PAIRS + 1, BLOCK, SLAB)] * 4,
                *[plane(BASES, 256, 256)] * 4,
                plane(BLOCK, WIDTH + 2 * SLAB, dtype=F32),
                plane(16, WIDTH, dtype=F32),
                plane(8, SLAB, dtype=F32),
                plane(4, 8, SLAB, dtype=F32),
                plane(8, 8, SLAB, dtype=F32),
                *[plane(NT, BLOCK, SLAB)] * 4,
                *[plane(PAD + ROWS + 8, SLAB, dtype=F32)] * 2,
                plane(LANCZOS, ROWS, SLAB, dtype=F32),
                *[plane(8, NV, 16, SLAB)] * 2,
                *[plane(NV, 8, 16, SLAB)] * 2,
                plane(8, 16, SLAB, dtype=F32),
                *[plane(NT, 16, SLAB)] * 2,
                pltpu.SemaphoreType.DMA((9,)),
                pltpu.SemaphoreType.DMA((2, CHUNKS)),
                pltpu.SemaphoreType.DMA((2, CHUNKS)),
                pltpu.SemaphoreType.DMA((10,)),
                pltpu.SemaphoreType.DMA((10,)),
            ],
            compiler_params=pltpu.CompilerParams(
                collective_id=0, has_side_effects=True, vmem_limit_bytes=60 * 2**20
            ),
        )(image, variance, mask, shift, coef, vert, horiz,
          jnp.transpose(colw, (1, 0, 2)), coloff, jnp.transpose(roww, (1, 0, 2)))
        both = both.astype(F32)
        return both[:BLOCK], both[BLOCK:]

    placed = (
        P("visit", "tile", None),
        P("visit", "tile", None),
        P("visit", "tile"),
        P("visit"),
        P("visit", None),
        P(),
        P(),
        P("visit", None, None),
        P("visit", None),
        P("visit", None, "tile"),
    )
    return jax.shard_map(
        body,
        mesh=mesh,
        in_specs=placed,
        out_specs=(P("tile", None), P("tile", None)),
        check_vma=False,
    )
```

```python
import jax
import jax.numpy as jnp
from jax import lax
from jax.experimental import pallas as pl
from jax.experimental.pallas import tpu as pltpu
from jax.sharding import PartitionSpec as P

MESH = pl.DeviceIdType.MESH
F32 = jnp.float32
BF16 = jnp.bfloat16
TAPS = 21
RIM = 10
BASES = 5
LANCZOS = 6
BLOCK = 32
SLAB = 128
PAD = 520
NV = 8
NT = 32
ROWS = NT * BLOCK
WIDTH = NT * SLAB
PAIRS = NT // 2
CHUNKS = 4
SPAN = WIDTH // CHUNKS
HALF = WIDTH // 2


def split(x):
    high = x.astype(BF16)
    return high, (x - high.astype(F32)).astype(BF16)


def cols(j, n=SLAB):
    return pl.ds(pl.multiple_of(j * n, n), n)


def far_first(n):
    return sorted(range(n), key=lambda gap: -min(gap, n - gap))


def kernel(
    image_hbm, variance_hbm, mask_hbm, shift, coef_hbm, vert_hbm, horiz_hbm, colw_hbm, coloff_hbm, roww_hbm,
    final,
    mask, coef, vert, horiz, colw, coloff, roww,
    image, variance,
    x_cat, v_mat, e_hi, e_lo, o_hi, o_lo, t_main_hi, t_main_lo, t_halo_hi, t_halo_lo,
    matched, factor, rw_mine, rw_quad, rw_all, s_iv, r_iv, s_cw, r_cw, ivf, cwf, wbi,
    nb_iv, nb_nu, c2_iv, c2_nu, total_iv, c3_iv, c3_nu,
    in_sem, halo_send, halo_recv, send_sem, recv_sem,
):
    v, t = lax.axis_index("visit"), lax.axis_index("tile")
    f_nu, f_iv = final.at[pl.ds(0, BLOCK)], final.at[pl.ds(BLOCK, BLOCK)]
    x, z = lax.div(t, 8), lax.rem(t, 8)
    y, core = lax.div(v, 2), lax.rem(v, 2)
    side = lax.div(t, NT // 2)
    to_self = (side == core) & (lax.rem(16 - 2 * z, 4) == y)

    get_image = pltpu.make_async_copy(image_hbm.at[0], image, in_sem.at[0])
    get_variance = pltpu.make_async_copy(variance_hbm.at[0], variance, in_sem.at[1])
    get_image.start()
    small = [
        pltpu.make_async_copy(source, target, in_sem.at[i + 2])
        for i, (source, target) in enumerate((
            (mask_hbm, mask), (roww_hbm, roww), (coef_hbm, coef), (vert_hbm, vert),
            (horiz_hbm, horiz), (colw_hbm, colw), (coloff_hbm, coloff)))
    ]
    for get in small:
        get.start()
    get_variance.start()

    barrier = pltpu.get_barrier_semaphore()

    def greet(v2, t2):
        pl.semaphore_signal(barrier, inc=1, device_id=(v2, t2), device_id_type=MESH)

    x_at = [8 * lax.rem(x + gap, 4) for gap in range(4)]
    z_at = [lax.rem(z + gap, 8) for gap in range(8)]
    y_at = [2 * lax.rem(y + gap, 4) for gap in range(4)]
    tiles = sorted(((dx, dz) for dx in range(4) for dz in range(8)), key=lambda gap: -min(gap[0], 4 - gap[0]) - min(gap[1], 8 - gap[1]))
    for dx, dz in tiles[:-1]:
        greet(v, x_at[dx] + z_at[dz])
    other = 1 - core
    for gap in (2, 1, 3):
        greet(y_at[gap] + core, t)
        greet(y_at[gap] + other, t)
    greet(y_at[0] + other, t)

    get_image.wait()

    def fill(j, c):
        x_cat[16:48, cols(j, 512)] = image[:, cols(j, 512)].astype(BF16)
        return c

    lax.fori_loop(0, WIDTH // 512, fill, 0)
    pl.semaphore_wait(barrier, (NT - 1) + (NV - 1))

    def halo(way, g):
        from_row, to_row, t2 = ((32, 0, lax.rem(t + 1, NT)), (16, 48, lax.rem(t + NT - 1, NT)))[way]
        return pltpu.make_async_remote_copy(
            src_ref=x_cat.at[pl.ds(from_row, 16), cols(g, SPAN)], dst_ref=x_cat.at[pl.ds(to_row, 16), cols(g, SPAN)],
            send_sem=halo_send.at[way, g], recv_sem=halo_recv.at[way, g],
            device_id=(v, t2), device_id_type=MESH)

    def start_halo(g, c):
        halo(0, g).start()
        halo(1, g).start()
        return c

    lax.fori_loop(0, CHUNKS, start_halo, 0)

    def fill_low(j, c):
        high = x_cat[16:48, cols(j, 512)]
        x_cat[112:144, cols(j, 512)] = high
        x_cat[64:96, cols(j, 512)] = (image[:, cols(j, 512)] - high.astype(F32)).astype(BF16)
        return c


    def send(source, target, at, v2, t2):
        pltpu.make_async_remote_copy(
            src_ref=source, dst_ref=target, send_sem=send_sem.at[at], recv_sem=recv_sem.at[at],
            device_id=(v2, t2), device_id_type=MESH).start()

    def arrived(ref, at):
        pltpu.make_async_copy(ref, ref, recv_sem.at[at]).wait()

    def left(ref, at):
        pltpu.make_async_copy(ref, ref, send_sem.at[at]).wait()

    for get in small:
        get.wait()
    rw_mine[...] = jnp.zeros_like(rw_mine)
    for q in range(4):
        for k in range(LANCZOS):
            rw_mine[k:k + 1, BLOCK * q:BLOCK * (q + 1)] = roww[k]
    lane = lax.broadcasted_iota(jnp.int32, (8, SLAB), 1)
    rw_mine[...] = jnp.where(lax.div(lane, BLOCK) == x, rw_mine[...], 0.0)
    for dx in (2, 1, 3):
        send(rw_mine, rw_quad.at[x], 6, v, x_at[dx] + z)
    rw_quad[x] = rw_mine[...]

    flags = jnp.broadcast_to(mask[...].astype(F32), (BLOCK, BLOCK))
    same = lax.broadcasted_iota(jnp.int32, (BLOCK, BLOCK), 0) == lax.broadcasted_iota(jnp.int32, (BLOCK, BLOCK), 1)
    usable = jnp.sum(jnp.where(same, flags, 0.0), axis=1, keepdims=True)
    get_variance.wait()

    def weigh(j, c):
        s_iv[j] = (usable / variance[:, cols(j)]).astype(BF16)
        return c

    lax.fori_loop(0, NT, weigh, 0)

    for dx, dz in tiles[:-1]:
        t2 = x_at[dx] + z_at[dz]
        send(s_iv.at[t2], r_iv.at[t], 0, v, t2)
    r_iv[t] = s_iv[t]
    lax.fori_loop(0, WIDTH // 512, fill_low, 0)

    r_at = lax.broadcasted_iota(jnp.int32, (BLOCK, 160), 0)
    q_at = lax.broadcasted_iota(jnp.int32, (BLOCK, 160), 1)
    q_row = jnp.where(q_at < 64, q_at - 16, jnp.where(q_at < 96, q_at - 64, q_at - 112))
    tap = q_row - r_at + RIM
    for b in range(BASES):
        value = jnp.zeros((BLOCK, 160), F32)
        for i in range(TAPS):
            value = jnp.where(tap == i, coef[0, b] * vert[b, i], value)
        high = value.astype(BF16).astype(F32)
        v_mat[BLOCK * b:BLOCK * (b + 1), :] = jnp.where(q_at < 96, high, value - high).astype(BF16)

    n_at = lax.broadcasted_iota(jnp.int32, (16, 256), 1)
    k_at = lax.broadcasted_iota(jnp.int32, (16, 256), 0)

    def band(d):
        values = [jnp.zeros((16, 256), F32) for _ in range(BASES)]
        for i in range(TAPS):
            hit = d == i
            values = [jnp.where(hit, horiz[b, i], values[b]) for b in range(BASES)]
        return [split(value) for value in values]

    def build(c, carry):
        parts = band(16 * c + k_at - n_at + RIM)
        at = pl.ds(pl.multiple_of(16 * c, 16), 16)
        for b in range(BASES):
            t_main_hi[b, at, :], t_main_lo[b, at, :] = parts[b]
            t_halo_hi[b, at, :] = jnp.zeros((16, 256), BF16)
            t_halo_lo[b, at, :] = jnp.zeros((16, 256), BF16)
        return carry

    lax.fori_loop(0, 16, build, 0)
    for start, gap in ((112, -118), (128, 138)):
        parts = band(start + k_at - n_at + gap)
        for b in range(BASES):
            t_halo_hi[b, start:start + 16, :], t_halo_lo[b, start:start + 16, :] = parts[b]

    c_at = lax.broadcasted_iota(jnp.int32, (1, 512), 1)

    def weights(g, c):
        delta = coloff[0:1, cols(g, 512)] - (c_at + 512 * g)
        sums = [jnp.zeros((1, 512), F32) for _ in range(11)]
        for gap in range(-5, 1):
            hit = delta == gap
            for k in range(LANCZOS):
                sums[gap + k + 5] = sums[gap + k + 5] + jnp.where(hit, colw[k, :, cols(g, 512)], 0.0)
        for d in range(11):
            factor[d:d + 1, cols(g, 512)] = sums[d]
        return c

    lax.fori_loop(0, WIDTH // 512, weights, 0)

    for ref in (e_hi, e_lo):
        ref[:, PAIRS] = jnp.zeros((BASES, BLOCK, SLAB), BF16)
    for ref in (o_hi, o_lo):
        ref[:, 0] = jnp.zeros((BASES, BLOCK, SLAB), BF16)
    matched[:, 0:SLAB] = jnp.zeros((BLOCK, SLAB), F32)
    matched[:, SLAB + WIDTH:] = jnp.zeros((BLOCK, SLAB), F32)
    for ref in (ivf, cwf):
        ref[0:PAD, :] = jnp.zeros((PAD, SLAB), F32)
        ref[PAD + ROWS:, :] = jnp.zeros((8, SLAB), F32)

    arrived(rw_quad.at[pl.ds(0, 3)], 6)
    rw_all[z] = rw_quad[0] + rw_quad[1] + rw_quad[2] + rw_quad[3]
    for dz in far_first(8)[:-1]:
        send(rw_all.at[z], rw_all.at[z], 7, v, 8 * x + z_at[dz])

    def vertical(g):
        for way in range(2):
            halo(way, g).wait_recv()

        @pl.when(t == 0)
        def _():
            x_cat[0:16, cols(g, SPAN)] = jnp.zeros((16, SPAN), BF16)

        @pl.when(t == NT - 1)
        def _():
            x_cat[48:64, cols(g, SPAN)] = jnp.zeros((16, SPAN), BF16)

        x_cat[96:112, cols(g, SPAN)] = x_cat[0:16, cols(g, SPAN)]
        x_cat[144:160, cols(g, SPAN)] = x_cat[48:64, cols(g, SPAN)]

        passed = jnp.dot(v_mat[...], x_cat[:, cols(g, SPAN)], preferred_element_type=F32)
        for i in range(4):
            j = 4 * g + i
            for b in range(BASES):
                high, low = split(passed[BLOCK * b:BLOCK * (b + 1), 256 * i:256 * (i + 1)])
                e_hi[b, j], o_hi[b, j + 1] = high[:, :SLAB], high[:, SLAB:]
                e_lo[b, j], o_lo[b, j + 1] = low[:, :SLAB], low[:, SLAB:]

    def horizontal(g):
        def part(ref, b, start):
            return ref[b, pl.ds(4 * g + start, 4)].reshape(4 * BLOCK, SLAB)

        total = jnp.zeros((4 * BLOCK, 256), F32)
        for b in range(BASES):
            main_hi = jnp.concatenate([part(e_hi, b, 0), part(o_hi, b, 1)], axis=1)
            main_lo = jnp.concatenate([part(e_lo, b, 0), part(o_lo, b, 1)], axis=1)
            halo_hi = jnp.concatenate([part(o_hi, b, 0), part(e_hi, b, 1)], axis=1)
            halo_lo = jnp.concatenate([part(o_lo, b, 0), part(e_lo, b, 1)], axis=1)
            for data, matrix in (
                (main_hi, t_main_hi), (main_lo, t_main_hi), (main_hi, t_main_lo),
                (halo_hi, t_halo_hi), (halo_lo, t_halo_hi), (halo_hi, t_halo_lo),
            ):
                total = total + jnp.dot(data, matrix[b], preferred_element_type=F32)
        for i in range(4):
            at = pl.ds(pl.multiple_of(SPAN * g + 256 * i + SLAB, SLAB), 256)
            matched[:, at] = total[BLOCK * i:BLOCK * (i + 1)]

    def interpolate(g):
        def step(i, c):
            j = 2 * g + i
            for r in range(2):
                window = matched[16 * r:16 * (r + 1), pl.ds(pl.multiple_of(512 * j, 512), 768)]
                total = jnp.zeros((16, 512), F32)
                for d in range(-5, 6):
                    moved = pltpu.roll(window, (-d) % 768, 1) if d else window
                    total = total + factor[d + 5:d + 6, cols(j, 512)] * moved[:, SLAB:SLAB + 512]
                total = total.astype(BF16)
                for q in range(4):
                    s_cw[4 * j + q, 16 * r:16 * (r + 1), :] = total[:, SLAB * q:SLAB * (q + 1)]
            return c

        lax.fori_loop(0, 2, step, 0)

    def send_cw(g):
        for dz in far_first(8)[:-1]:
            t2 = 8 * g + z_at[dz]
            send(s_cw.at[t2], r_cw.at[t], 1, v, t2)

        @pl.when(g != x)
        def _():
            send(s_cw.at[8 * g + z], r_cw.at[t], 1, v, 8 * g + z)

    def chunk(s, c):
        @pl.when(s < CHUNKS)
        def _():
            vertical(s)

        @pl.when((s >= 1) & (s < CHUNKS + 1))
        def _():
            horizontal(s - 1)

        @pl.when(s >= 2)
        def _():
            interpolate(s - 2)
            send_cw(s - 2)

        return c

    lax.fori_loop(0, CHUNKS + 2, chunk, 0)
    r_cw[t] = s_cw[t]

    def unpack(ref, target):
        def step(j, c):
            target[pl.ds(pl.multiple_of(PAD + BLOCK * j, 8), BLOCK), :] = ref[j].astype(F32)
            return c

        lax.fori_loop(0, NT, step, 0)

    def share(ref, x2, z2, plane):
        u2 = 2 * lax.rem(x2 + 24 - z2 - x - z, 4)
        ref[z2, pl.ds(u2, 2)] = plane.astype(BF16).reshape(2, 16, SLAB)

    def rows_of(x2, z2):
        return 8 * BLOCK * x2 + pl.multiple_of(BLOCK * z2, BLOCK)

    arrived(r_iv.at[pl.ds(0, NT - 1)], 0)
    arrived(rw_all.at[pl.ds(0, 7)], 7)
    unpack(r_iv, ivf)
    amount = shift[0]
    pick = lax.broadcasted_iota(jnp.int32, (16, LANCZOS * SLAB), 0)
    pick = lax.rem(pick, 8) == lax.div(lax.broadcasted_iota(jnp.int32, (16, LANCZOS * SLAB), 1), SLAB)
    pick = pick.astype(F32).astype(BF16)
    row_at = lax.broadcasted_iota(jnp.int32, (BLOCK, SLAB), 0)

    def spread(z2, c):
        whole = rw_all[z2]
        high = whole.astype(BF16).astype(F32)
        joined = jnp.concatenate([high, whole - high], axis=0).astype(BF16)
        wide = lax.dot_general(joined, pick, (((0,), (0,)), ((), ())), preferred_element_type=F32)
        for x2 in range(4):
            start = rows_of(x2, z2)
            sky = ivf[pl.ds(start + PAD - amount, BLOCK), :]
            share(nb_iv, x2, z2, sky)
            for k in range(LANCZOS):
                inside = row_at + (start + k - 2) < ROWS
                weight = wide[BLOCK * x2:BLOCK * (x2 + 1), SLAB * k:SLAB * (k + 1)]
                wbi[k, pl.ds(start, BLOCK), :] = jnp.where(inside, weight * sky, 0.0)
        return c

    lax.fori_loop(0, 8, spread, 0)

    first = 1 - lax.div(z, 4)

    def half(h):
        return pl.ds(4 * h, 4)

    def scatter(source, target, at, h):
        for gap in (2, 1, 3, 0):
            for seat in (core, other) if gap else (other,):
                v2 = y_at[gap] + seat
                send(source.at[half(h), v2], target.at[v, half(h)], at, v2, t)
        target[v, half(h)] = source[half(h), v]

    def deliver(source, target, at, h, own):
        rows, columns = pl.ds(pl.multiple_of(16 * core, 16), 16), cols(t)
        for turn in (2, 1, 3, 0) if own else (0, 1, 3, 2):
            z2 = 4 * h + lax.rem(z + turn, 4)
            t2 = 8 * lax.rem(y + z2 + x + z, 4) + z2
            for gap in (2, 1, 3):
                send(source.at[z2], target.at[rows, columns], at, y_at[gap] + side, t2)
            if turn or not own:
                send(source.at[z2], target.at[rows, columns], at, y_at[0] + side, t2)
        if not own:
            return
        me = (side == core) & (t2 == t)

        @pl.when(jnp.logical_not(me))
        def _():
            send(source.at[z], target.at[rows, columns], at, y_at[0] + side, t2)

        @pl.when(me)
        def _():
            pltpu.make_async_copy(source.at[z], target.at[rows, columns], recv_sem.at[at]).start()

    def swap(target, at):
        mine = target.at[:, cols(core, HALF)]
        send(mine, mine, at, v + 1 - 2 * core, t)

    def summed(ref, i):
        total = ref[0, i].astype(F32)
        for u in range(1, NV):
            total = total + ref[u, i].astype(F32)
        return total

    for h, at in ((first, 2), (1 - first, 10)):
        scatter(nb_iv, c2_iv, at, h)

    arrived(r_cw.at[pl.ds(0, NT - 1)], 1)
    unpack(r_cw, cwf)

    def warp(z2, c):
        for x2 in range(4):
            start = rows_of(x2, z2)
            total = jnp.zeros((BLOCK, SLAB), F32)
            for k in range(LANCZOS):
                total = total + wbi[k, pl.ds(start, BLOCK), :] * cwf[pl.ds(start + PAD + k - 2 - amount, BLOCK), :]
            share(nb_nu, x2, z2, total)
        return c

    for h, at in ((first, 3), (1 - first, 11)):
        lax.fori_loop(4 * h, 4 * h + 4, warp, 0)
        scatter(nb_nu, c2_nu, at, h)

    def add_iv(i, c):
        total = summed(c2_iv, i)
        total_iv[i] = total
        c3_iv[i] = total.astype(BF16)
        return c

    for h, at, own in ((first, 2, False), (1 - first, 10, True)):
        arrived(c2_iv.at[pl.ds(0, NV - 1), half(0)], at)
        lax.fori_loop(4 * h, 4 * h + 4, add_iv, 0)
        deliver(c3_iv, f_iv, 4, h, own)

    def add_nu(i, c):
        c3_nu[i] = (summed(c2_nu, i) / jnp.maximum(total_iv[i], 1.0)).astype(BF16)
        return c

    for h, at, own in ((first, 3, False), (1 - first, 11, True)):
        arrived(c2_nu.at[pl.ds(0, NV - 1), half(0)], at)
        lax.fori_loop(4 * h, 4 * h + 4, add_nu, 0)
        deliver(c3_nu, f_nu, 5, h, own)

    arrived(f_iv.at[:, pl.ds(0, HALF)], 4)
    swap(f_iv, 8)
    arrived(f_nu.at[:, pl.ds(0, HALF)], 5)
    swap(f_nu, 9)

    def halo_left(g, c):
        halo(0, g).wait_send()
        halo(1, g).wait_send()
        return c

    lax.fori_loop(0, CHUNKS, halo_left, 0)
    left(rw_quad.at[pl.ds(0, 3)], 6)
    left(rw_all.at[pl.ds(0, 7)], 7)
    left(s_iv.at[pl.ds(0, NT - 1)], 0)
    left(s_cw.at[pl.ds(0, NT - 1)], 1)
    for target, at in ((c2_iv, 2), (c2_iv, 10), (c2_nu, 3), (c2_nu, 11)):
        left(target.at[pl.ds(0, NV - 1), half(0)], at)
    for c3, at in ((c3_iv, 4), (c3_nu, 5)):
        @pl.when(to_self)
        def _():
            left(c3.at[pl.ds(0, NT - 1)], at)

        @pl.when(jnp.logical_not(to_self))
        def _():
            left(c3, at)

    for target, at in ((f_iv, 8), (f_nu, 9)):
        left(target.at[:, pl.ds(0, HALF)], at)
        arrived(target.at[:, pl.ds(0, HALF)], at)


def solution(mesh):
    def body(image, variance, mask, shift, coef, vert, horiz, colw, coloff, roww):
        vmem = pl.BlockSpec(memory_space=pltpu.VMEM)
        smem = pl.BlockSpec(memory_space=pltpu.SMEM)
        hbm = pl.BlockSpec(memory_space=pltpu.HBM)

        def plane(*shape, dtype=BF16):
            return pltpu.VMEM(shape, dtype)

        def keep(array):
            return pltpu.with_memory_space_constraint(array, pltpu.HBM)

        both = pl.pallas_call(
            kernel,
            out_shape=jax.ShapeDtypeStruct((2 * BLOCK, WIDTH), BF16),
            in_specs=[hbm, hbm, hbm, smem, *[hbm] * 6],
            out_specs=vmem,
            scratch_shapes=[
                plane(1, BLOCK, dtype=jnp.int32),
                pltpu.SMEM((1, BASES), F32),
                pltpu.SMEM((BASES, TAPS), F32),
                pltpu.SMEM((BASES, TAPS), F32),
                plane(LANCZOS, 1, WIDTH, dtype=F32),
                plane(1, WIDTH, dtype=jnp.int32),
                plane(LANCZOS, 1, BLOCK, dtype=F32),
                *[plane(BLOCK, WIDTH, dtype=F32)] * 2,
                plane(160, WIDTH),
                plane(160, 160),
                *[plane(BASES, PAIRS + 1, BLOCK, SLAB)] * 4,
                *[plane(BASES, 256, 256)] * 4,
                plane(BLOCK, WIDTH + 2 * SLAB, dtype=F32),
                plane(16, WIDTH, dtype=F32),
                plane(8, SLAB, dtype=F32),
                plane(4, 8, SLAB, dtype=F32),
                plane(8, 8, SLAB, dtype=F32),
                *[plane(NT, BLOCK, SLAB)] * 4,
                *[plane(PAD + ROWS + 8, SLAB, dtype=F32)] * 2,
                plane(LANCZOS, ROWS, SLAB, dtype=F32),
                *[plane(8, NV, 16, SLAB)] * 2,
                *[plane(NV, 8, 16, SLAB)] * 2,
                plane(8, 16, SLAB, dtype=F32),
                *[plane(NT, 16, SLAB)] * 2,
                pltpu.SemaphoreType.DMA((9,)),
                pltpu.SemaphoreType.DMA((2, CHUNKS)),
                pltpu.SemaphoreType.DMA((2, CHUNKS)),
                pltpu.SemaphoreType.DMA((12,)),
                pltpu.SemaphoreType.DMA((12,)),
            ],
            compiler_params=pltpu.CompilerParams(
                collective_id=0, has_side_effects=True, vmem_limit_bytes=48 * 2**20
            ),
        )(keep(image), keep(variance), keep(mask), shift, keep(coef), keep(vert), keep(horiz),
          keep(jnp.transpose(colw, (1, 0, 2))), keep(coloff), keep(jnp.transpose(roww, (1, 0, 2))))
        both = both.astype(F32)
        return both[:BLOCK], both[BLOCK:]

    placed = (
        P("visit", "tile", None),
        P("visit", "tile", None),
        P("visit", "tile"),
        P("visit"),
        P("visit", None),
        P(),
        P(),
        P("visit", None, None),
        P("visit", None),
        P("visit", None, "tile"),
    )
    return jax.shard_map(
        body,
        mesh=mesh,
        in_specs=placed,
        out_specs=(P("tile", None), P("tile", None)),
        check_vma=False,
    )
```

```python
import jax
import jax.numpy as jnp
from jax import lax
from jax.experimental import pallas as pl
from jax.experimental.pallas import tpu as pltpu
from jax.sharding import PartitionSpec as P

MESH = pl.DeviceIdType.MESH
F32 = jnp.float32
BF16 = jnp.bfloat16
TAPS = 21
RIM = 10
BASES = 5
LANCZOS = 6
BLOCK = 32
SLAB = 128
PAD = 520
NV = 8
NT = 32
ROWS = NT * BLOCK
WIDTH = NT * SLAB
PAIRS = NT // 2
CHUNKS = 4
SPAN = WIDTH // CHUNKS
HALF = WIDTH // 2
FOLD = SPAN * RIM // 16


def split(x):
    high = x.astype(BF16)
    return high, (x - high.astype(F32)).astype(BF16)


def cols(j, n=SLAB):
    return pl.ds(pl.multiple_of(j * n, n), n)


def far_first(n):
    return sorted(range(n), key=lambda gap: -min(gap, n - gap))


def kernel(
    image_hbm, variance_hbm, mask_hbm, shift, coef_hbm, vert_hbm, horiz_hbm, colw_hbm, coloff_hbm, roww_hbm,
    final,
    mask, coef, vert, horiz, colw, coloff, roww,
    image, variance, folded, opened, h_send, h_recv,
    x_cat, v_mat, e_hi, e_lo, o_hi, o_lo, t_main_hi, t_main_lo, t_halo_hi, t_halo_lo,
    matched, factor, rw_mine, rw_quad, rw_all, s_iv, r_iv, s_cw, r_cw, ivf, cwf, wbi,
    nb_iv, nb_nu, c2_iv, c2_nu, total_iv, c3_iv, c3_nu,
    in_sem, halo_send, halo_recv, send_sem, recv_sem,
):
    v, t = lax.axis_index("visit"), lax.axis_index("tile")
    f_nu, f_iv = final.at[pl.ds(0, BLOCK)], final.at[pl.ds(BLOCK, BLOCK)]
    x, z = lax.div(t, 8), lax.rem(t, 8)
    y, core = lax.div(v, 2), lax.rem(v, 2)
    side = lax.div(t, NT // 2)
    to_self = (side == core) & (lax.rem(16 - 2 * z, 4) == y)

    get_image = pltpu.make_async_copy(image_hbm.at[0], image, in_sem.at[0])
    get_variance = pltpu.make_async_copy(variance_hbm.at[0], variance, in_sem.at[1])
    get_image.start()
    small = [
        pltpu.make_async_copy(source, target, in_sem.at[i + 2])
        for i, (source, target) in enumerate((
            (mask_hbm, mask), (roww_hbm, roww), (coef_hbm, coef), (vert_hbm, vert),
            (horiz_hbm, horiz), (colw_hbm, colw), (coloff_hbm, coloff)))
    ]
    for get in small:
        get.start()
    get_variance.start()

    barrier = pltpu.get_barrier_semaphore()

    def greet(v2, t2):
        pl.semaphore_signal(barrier, inc=1, device_id=(v2, t2), device_id_type=MESH)

    x_at = [8 * lax.rem(x + gap, 4) for gap in range(4)]
    z_at = [lax.rem(z + gap, 8) for gap in range(8)]
    y_at = [2 * lax.rem(y + gap, 4) for gap in range(4)]
    tiles = sorted(((dx, dz) for dx in range(4) for dz in range(8)), key=lambda gap: -min(gap[0], 4 - gap[0]) - min(gap[1], 8 - gap[1]))
    for dx, dz in tiles[:-1]:
        greet(v, x_at[dx] + z_at[dz])
    other = 1 - core
    for gap in (2, 1, 3):
        greet(y_at[gap] + core, t)
        greet(y_at[gap] + other, t)
    greet(y_at[0] + other, t)

    get_image.wait()

    def folds(row):
        return (
            (slice(row, row + 10), 0, slice(0, 10), 0, FOLD),
            (slice(row, row + 6), FOLD, slice(10, 16), 0, 384),
            (slice(row + 6, row + 10), FOLD, slice(10, 14), 384, 256),
            (slice(row + 6, row + 8), FOLD + 256, slice(14, 16), 384, 128),
            (slice(row + 8, row + 10), FOLD + 256, slice(14, 16), 512, 128),
        )

    def pack(g, c):
        for way, row in ((0, BLOCK - RIM), (1, 0)):
            for rows, start, to_rows, to_start, size in folds(row):
                at = pl.ds(pl.multiple_of(SPAN * g + start, SLAB), size)
                folded[to_rows, to_start:to_start + size] = image[rows, at]
            h_send[way, g] = folded[...].astype(BF16)
        return c

    lax.fori_loop(0, CHUNKS, pack, 0)
    pl.semaphore_wait(barrier, (NT - 1) + (NV - 1))

    def halo(way, g):
        return pltpu.make_async_remote_copy(
            src_ref=h_send.at[way, g], dst_ref=h_recv.at[way, g],
            send_sem=halo_send.at[way, g], recv_sem=halo_recv.at[way, g],
            device_id=(v, lax.rem(t + (1, NT - 1)[way], NT)), device_id_type=MESH)

    def start_halo(g, c):
        halo(0, g).start()
        halo(1, g).start()
        return c

    lax.fori_loop(0, CHUNKS, start_halo, 0)

    def fill_low(j, c):
        high = image[:, cols(j, 512)].astype(BF16)
        x_cat[16:48, cols(j, 512)] = high
        x_cat[112:144, cols(j, 512)] = high
        x_cat[64:96, cols(j, 512)] = (image[:, cols(j, 512)] - high.astype(F32)).astype(BF16)
        return c


    def send(source, target, at, v2, t2):
        pltpu.make_async_remote_copy(
            src_ref=source, dst_ref=target, send_sem=send_sem.at[at], recv_sem=recv_sem.at[at],
            device_id=(v2, t2), device_id_type=MESH).start()

    def arrived(ref, at):
        pltpu.make_async_copy(ref, ref, recv_sem.at[at]).wait()

    def left(ref, at):
        pltpu.make_async_copy(ref, ref, send_sem.at[at]).wait()

    for get in small:
        get.wait()
    rw_mine[...] = jnp.zeros_like(rw_mine)
    for q in range(4):
        for k in range(LANCZOS):
            rw_mine[k:k + 1, BLOCK * q:BLOCK * (q + 1)] = roww[k]
    lane = lax.broadcasted_iota(jnp.int32, (8, SLAB), 1)
    rw_mine[...] = jnp.where(lax.div(lane, BLOCK) == x, rw_mine[...], 0.0)
    for dx in (2, 1, 3):
        send(rw_mine, rw_quad.at[x], 6, v, x_at[dx] + z)
    rw_quad[x] = rw_mine[...]

    flags = jnp.broadcast_to(mask[...].astype(F32), (BLOCK, BLOCK))
    same = lax.broadcasted_iota(jnp.int32, (BLOCK, BLOCK), 0) == lax.broadcasted_iota(jnp.int32, (BLOCK, BLOCK), 1)
    usable = jnp.sum(jnp.where(same, flags, 0.0), axis=1, keepdims=True)
    get_variance.wait()

    def weigh(j, c):
        s_iv[j] = (usable / variance[:, cols(j)]).astype(BF16)
        return c

    lax.fori_loop(0, NT, weigh, 0)

    for dx, dz in tiles[:-1]:
        t2 = x_at[dx] + z_at[dz]
        send(s_iv.at[t2], r_iv.at[t], 0, v, t2)
    r_iv[t] = s_iv[t]
    lax.fori_loop(0, WIDTH // 512, fill_low, 0)

    r_at = lax.broadcasted_iota(jnp.int32, (BLOCK, 160), 0)
    q_at = lax.broadcasted_iota(jnp.int32, (BLOCK, 160), 1)
    q_row = jnp.where(q_at < 64, q_at - 16, jnp.where(q_at < 96, q_at - 64, q_at - 112))
    tap = q_row - r_at + RIM
    for b in range(BASES):
        value = jnp.zeros((BLOCK, 160), F32)
        for i in range(TAPS):
            value = jnp.where(tap == i, coef[0, b] * vert[b, i], value)
        high = value.astype(BF16).astype(F32)
        v_mat[BLOCK * b:BLOCK * (b + 1), :] = jnp.where(q_at < 96, high, value - high).astype(BF16)

    n_at = lax.broadcasted_iota(jnp.int32, (16, 256), 1)
    k_at = lax.broadcasted_iota(jnp.int32, (16, 256), 0)

    def band(d):
        values = [jnp.zeros((16, 256), F32) for _ in range(BASES)]
        for i in range(TAPS):
            hit = d == i
            values = [jnp.where(hit, horiz[b, i], values[b]) for b in range(BASES)]
        return [split(value) for value in values]

    def build(c, carry):
        parts = band(16 * c + k_at - n_at + RIM)
        at = pl.ds(pl.multiple_of(16 * c, 16), 16)
        for b in range(BASES):
            t_main_hi[b, at, :], t_main_lo[b, at, :] = parts[b]
            t_halo_hi[b, at, :] = jnp.zeros((16, 256), BF16)
            t_halo_lo[b, at, :] = jnp.zeros((16, 256), BF16)
        return carry

    lax.fori_loop(0, 16, build, 0)
    for start, gap in ((112, -118), (128, 138)):
        parts = band(start + k_at - n_at + gap)
        for b in range(BASES):
            t_halo_hi[b, start:start + 16, :], t_halo_lo[b, start:start + 16, :] = parts[b]

    c_at = lax.broadcasted_iota(jnp.int32, (1, 512), 1)

    def weights(g, c):
        delta = coloff[0:1, cols(g, 512)] - (c_at + 512 * g)
        sums = [jnp.zeros((1, 512), F32) for _ in range(11)]
        for gap in range(-5, 1):
            hit = delta == gap
            for k in range(LANCZOS):
                sums[gap + k + 5] = sums[gap + k + 5] + jnp.where(hit, colw[k, :, cols(g, 512)], 0.0)
        for d in range(11):
            factor[d:d + 1, cols(g, 512)] = sums[d]
        return c

    lax.fori_loop(0, WIDTH // 512, weights, 0)

    for ref in (e_hi, e_lo):
        ref[:, PAIRS] = jnp.zeros((BASES, BLOCK, SLAB), BF16)
    for ref in (o_hi, o_lo):
        ref[:, 0] = jnp.zeros((BASES, BLOCK, SLAB), BF16)
    matched[:, 0:SLAB] = jnp.zeros((BLOCK, SLAB), F32)
    matched[:, SLAB + WIDTH:] = jnp.zeros((BLOCK, SLAB), F32)
    for ref in (ivf, cwf):
        ref[0:PAD, :] = jnp.zeros((PAD, SLAB), F32)
        ref[PAD + ROWS:, :] = jnp.zeros((8, SLAB), F32)

    arrived(rw_quad.at[pl.ds(0, 3)], 6)
    rw_all[z] = rw_quad[0] + rw_quad[1] + rw_quad[2] + rw_quad[3]
    for dz in far_first(8)[:-1]:
        send(rw_all.at[z], rw_all.at[z], 7, v, 8 * x + z_at[dz])

    def vertical(g):
        for way in range(2):
            halo(way, g).wait_recv()

        for way, row, present, first_row, second_row in ((0, 6, t > 0, 0, 96), (1, 0, t < NT - 1, 48, 144)):
            folded[...] = h_recv[way, g].astype(F32)
            opened[...] = jnp.zeros_like(opened)
            for rows, start, from_rows, from_start, size in folds(row):
                opened[rows, start:start + size] = folded[from_rows, from_start:from_start + size]
            near = jnp.where(present, opened[...], 0.0).astype(BF16)
            x_cat[first_row:first_row + 16, cols(g, SPAN)] = near
            x_cat[second_row:second_row + 16, cols(g, SPAN)] = near

        passed = jnp.dot(v_mat[...], x_cat[:, cols(g, SPAN)], preferred_element_type=F32)
        for i in range(4):
            j = 4 * g + i
            for b in range(BASES):
                high, low = split(passed[BLOCK * b:BLOCK * (b + 1), 256 * i:256 * (i + 1)])
                e_hi[b, j], o_hi[b, j + 1] = high[:, :SLAB], high[:, SLAB:]
                e_lo[b, j], o_lo[b, j + 1] = low[:, :SLAB], low[:, SLAB:]

    def horizontal(g):
        def part(ref, b, start):
            return ref[b, pl.ds(4 * g + start, 4)].reshape(4 * BLOCK, SLAB)

        total = jnp.zeros((4 * BLOCK, 256), F32)
        for b in range(BASES):
            main_hi = jnp.concatenate([part(e_hi, b, 0), part(o_hi, b, 1)], axis=1)
            main_lo = jnp.concatenate([part(e_lo, b, 0), part(o_lo, b, 1)], axis=1)
            halo_hi = jnp.concatenate([part(o_hi, b, 0), part(e_hi, b, 1)], axis=1)
            halo_lo = jnp.concatenate([part(o_lo, b, 0), part(e_lo, b, 1)], axis=1)
            for data, matrix in (
                (main_hi, t_main_hi), (main_lo, t_main_hi), (main_hi, t_main_lo),
                (halo_hi, t_halo_hi), (halo_lo, t_halo_hi), (halo_hi, t_halo_lo),
            ):
                total = total + jnp.dot(data, matrix[b], preferred_element_type=F32)
        for i in range(4):
            at = pl.ds(pl.multiple_of(SPAN * g + 256 * i + SLAB, SLAB), 256)
            matched[:, at] = total[BLOCK * i:BLOCK * (i + 1)]

    def interpolate(g):
        def step(i, c):
            j = 2 * g + i
            for r in range(2):
                window = matched[16 * r:16 * (r + 1), pl.ds(pl.multiple_of(512 * j, 512), 768)]
                total = jnp.zeros((16, 512), F32)
                for d in range(-5, 6):
                    moved = pltpu.roll(window, (-d) % 768, 1) if d else window
                    total = total + factor[d + 5:d + 6, cols(j, 512)] * moved[:, SLAB:SLAB + 512]
                total = total.astype(BF16)
                for q in range(4):
                    s_cw[4 * j + q, 16 * r:16 * (r + 1), :] = total[:, SLAB * q:SLAB * (q + 1)]
            return c

        lax.fori_loop(0, 2, step, 0)

    def send_cw(g):
        for dz in far_first(8)[:-1]:
            t2 = 8 * g + z_at[dz]
            send(s_cw.at[t2], r_cw.at[t], 1, v, t2)

        @pl.when(g != x)
        def _():
            send(s_cw.at[8 * g + z], r_cw.at[t], 1, v, 8 * g + z)

    def chunk(s, c):
        @pl.when(s < CHUNKS)
        def _():
            vertical(s)

        @pl.when((s >= 1) & (s < CHUNKS + 1))
        def _():
            horizontal(s - 1)

        @pl.when(s >= 2)
        def _():
            interpolate(s - 2)
            send_cw(s - 2)

        return c

    lax.fori_loop(0, CHUNKS + 2, chunk, 0)
    r_cw[t] = s_cw[t]

    def unpack(ref, target):
        def step(j, c):
            target[pl.ds(pl.multiple_of(PAD + BLOCK * j, 8), BLOCK), :] = ref[j].astype(F32)
            return c

        lax.fori_loop(0, NT, step, 0)

    def share(ref, x2, z2, plane):
        u2 = 2 * lax.rem(x2 + 24 - z2 - x - z, 4)
        ref[z2, pl.ds(u2, 2)] = plane.astype(BF16).reshape(2, 16, SLAB)

    def rows_of(x2, z2):
        return 8 * BLOCK * x2 + pl.multiple_of(BLOCK * z2, BLOCK)

    arrived(r_iv.at[pl.ds(0, NT - 1)], 0)
    arrived(rw_all.at[pl.ds(0, 7)], 7)
    unpack(r_iv, ivf)
    amount = shift[0]
    pick = lax.broadcasted_iota(jnp.int32, (16, LANCZOS * SLAB), 0)
    pick = lax.rem(pick, 8) == lax.div(lax.broadcasted_iota(jnp.int32, (16, LANCZOS * SLAB), 1), SLAB)
    pick = pick.astype(F32).astype(BF16)
    row_at = lax.broadcasted_iota(jnp.int32, (BLOCK, SLAB), 0)

    def spread(z2, c):
        whole = rw_all[z2]
        high = whole.astype(BF16).astype(F32)
        joined = jnp.concatenate([high, whole - high], axis=0).astype(BF16)
        wide = lax.dot_general(joined, pick, (((0,), (0,)), ((), ())), preferred_element_type=F32)
        for x2 in range(4):
            start = rows_of(x2, z2)
            sky = ivf[pl.ds(start + PAD - amount, BLOCK), :]
            share(nb_iv, x2, z2, sky)
            for k in range(LANCZOS):
                inside = row_at + (start + k - 2) < ROWS
                weight = wide[BLOCK * x2:BLOCK * (x2 + 1), SLAB * k:SLAB * (k + 1)]
                wbi[k, pl.ds(start, BLOCK), :] = jnp.where(inside, weight * sky, 0.0)
        return c

    lax.fori_loop(0, 8, spread, 0)

    first = 1 - lax.div(z, 4)

    def half(h):
        return pl.ds(4 * h, 4)

    def scatter(source, target, at, h):
        for gap in (2, 1, 3, 0):
            for seat in (core, other) if gap else (other,):
                v2 = y_at[gap] + seat
                send(source.at[half(h), v2], target.at[v, half(h)], at, v2, t)
        target[v, half(h)] = source[half(h), v]

    def deliver(source, target, at, h, own):
        rows, columns = pl.ds(pl.multiple_of(16 * core, 16), 16), cols(t)
        for turn in (2, 1, 3, 0) if own else (0, 1, 3, 2):
            z2 = 4 * h + lax.rem(z + turn, 4)
            t2 = 8 * lax.rem(y + z2 + x + z, 4) + z2
            for gap in (2, 1, 3):
                send(source.at[z2], target.at[rows, columns], at, y_at[gap] + side, t2)
            if turn or not own:
                send(source.at[z2], target.at[rows, columns], at, y_at[0] + side, t2)
        if not own:
            return
        me = (side == core) & (t2 == t)

        @pl.when(jnp.logical_not(me))
        def _():
            send(source.at[z], target.at[rows, columns], at, y_at[0] + side, t2)

        @pl.when(me)
        def _():
            pltpu.make_async_copy(source.at[z], target.at[rows, columns], recv_sem.at[at]).start()

    def swap(target, at):
        mine = target.at[:, cols(core, HALF)]
        send(mine, mine, at, v + 1 - 2 * core, t)

    def summed(ref, i):
        total = ref[0, i].astype(F32)
        for u in range(1, NV):
            total = total + ref[u, i].astype(F32)
        return total

    for h, at in ((first, 2), (1 - first, 10)):
        scatter(nb_iv, c2_iv, at, h)

    arrived(r_cw.at[pl.ds(0, NT - 1)], 1)
    unpack(r_cw, cwf)

    def warp(z2, c):
        for x2 in range(4):
            start = rows_of(x2, z2)
            total = jnp.zeros((BLOCK, SLAB), F32)
            for k in range(LANCZOS):
                total = total + wbi[k, pl.ds(start, BLOCK), :] * cwf[pl.ds(start + PAD + k - 2 - amount, BLOCK), :]
            share(nb_nu, x2, z2, total)
        return c

    for h, at in ((first, 3), (1 - first, 11)):
        lax.fori_loop(4 * h, 4 * h + 4, warp, 0)
        scatter(nb_nu, c2_nu, at, h)

    def add_iv(i, c):
        total = summed(c2_iv, i)
        total_iv[i] = total
        c3_iv[i] = total.astype(BF16)
        return c

    for h, at, own in ((first, 2, False), (1 - first, 10, True)):
        arrived(c2_iv.at[pl.ds(0, NV - 1), half(0)], at)
        lax.fori_loop(4 * h, 4 * h + 4, add_iv, 0)
        deliver(c3_iv, f_iv, 4, h, own)

    def add_nu(i, c):
        c3_nu[i] = (summed(c2_nu, i) / jnp.maximum(total_iv[i], 1.0)).astype(BF16)
        return c

    for h, at, own in ((first, 3, False), (1 - first, 11, True)):
        arrived(c2_nu.at[pl.ds(0, NV - 1), half(0)], at)
        lax.fori_loop(4 * h, 4 * h + 4, add_nu, 0)
        deliver(c3_nu, f_nu, 5, h, own)

    arrived(f_iv.at[:, pl.ds(0, HALF)], 4)
    swap(f_iv, 8)
    arrived(f_nu.at[:, pl.ds(0, HALF)], 5)
    swap(f_nu, 9)

    def halo_left(g, c):
        halo(0, g).wait_send()
        halo(1, g).wait_send()
        return c

    lax.fori_loop(0, CHUNKS, halo_left, 0)
    left(rw_quad.at[pl.ds(0, 3)], 6)
    left(rw_all.at[pl.ds(0, 7)], 7)
    left(s_iv.at[pl.ds(0, NT - 1)], 0)
    left(s_cw.at[pl.ds(0, NT - 1)], 1)
    for target, at in ((c2_iv, 2), (c2_iv, 10), (c2_nu, 3), (c2_nu, 11)):
        left(target.at[pl.ds(0, NV - 1), half(0)], at)
    for c3, at in ((c3_iv, 4), (c3_nu, 5)):
        @pl.when(to_self)
        def _():
            left(c3.at[pl.ds(0, NT - 1)], at)

        @pl.when(jnp.logical_not(to_self))
        def _():
            left(c3, at)

    for target, at in ((f_iv, 8), (f_nu, 9)):
        left(target.at[:, pl.ds(0, HALF)], at)
        arrived(target.at[:, pl.ds(0, HALF)], at)


def solution(mesh):
    def body(image, variance, mask, shift, coef, vert, horiz, colw, coloff, roww):
        vmem = pl.BlockSpec(memory_space=pltpu.VMEM)
        smem = pl.BlockSpec(memory_space=pltpu.SMEM)
        hbm = pl.BlockSpec(memory_space=pltpu.HBM)

        def plane(*shape, dtype=BF16):
            return pltpu.VMEM(shape, dtype)

        def keep(array):
            return pltpu.with_memory_space_constraint(array, pltpu.HBM)

        both = pl.pallas_call(
            kernel,
            out_shape=jax.ShapeDtypeStruct((2 * BLOCK, WIDTH), BF16),
            in_specs=[hbm, hbm, hbm, smem, *[hbm] * 6],
            out_specs=vmem,
            scratch_shapes=[
                plane(1, BLOCK, dtype=jnp.int32),
                pltpu.SMEM((1, BASES), F32),
                pltpu.SMEM((BASES, TAPS), F32),
                pltpu.SMEM((BASES, TAPS), F32),
                plane(LANCZOS, 1, WIDTH, dtype=F32),
                plane(1, WIDTH, dtype=jnp.int32),
                plane(LANCZOS, 1, BLOCK, dtype=F32),
                *[plane(BLOCK, WIDTH, dtype=F32)] * 2,
                plane(16, FOLD, dtype=F32),
                plane(16, SPAN, dtype=F32),
                *[plane(2, CHUNKS, 16, FOLD)] * 2,
                plane(160, WIDTH),
                plane(160, 160),
                *[plane(BASES, PAIRS + 1, BLOCK, SLAB)] * 4,
                *[plane(BASES, 256, 256)] * 4,
                plane(BLOCK, WIDTH + 2 * SLAB, dtype=F32),
                plane(16, WIDTH, dtype=F32),
                plane(8, SLAB, dtype=F32),
                plane(4, 8, SLAB, dtype=F32),
                plane(8, 8, SLAB, dtype=F32),
                *[plane(NT, BLOCK, SLAB)] * 4,
                *[plane(PAD + ROWS + 8, SLAB, dtype=F32)] * 2,
                plane(LANCZOS, ROWS, SLAB, dtype=F32),
                *[plane(8, NV, 16, SLAB)] * 2,
                *[plane(NV, 8, 16, SLAB)] * 2,
                plane(8, 16, SLAB, dtype=F32),
                *[plane(NT, 16, SLAB)] * 2,
                pltpu.SemaphoreType.DMA((9,)),
                pltpu.SemaphoreType.DMA((2, CHUNKS)),
                pltpu.SemaphoreType.DMA((2, CHUNKS)),
                pltpu.SemaphoreType.DMA((12,)),
                pltpu.SemaphoreType.DMA((12,)),
            ],
            compiler_params=pltpu.CompilerParams(
                collective_id=0, has_side_effects=True, vmem_limit_bytes=48 * 2**20
            ),
        )(keep(image), keep(variance), keep(mask), shift, keep(coef), keep(vert), keep(horiz),
          keep(jnp.transpose(colw, (1, 0, 2))), keep(coloff), keep(jnp.transpose(roww, (1, 0, 2))))
        both = both.astype(F32)
        return both[:BLOCK], both[BLOCK:]

    placed = (
        P("visit", "tile", None),
        P("visit", "tile", None),
        P("visit", "tile"),
        P("visit"),
        P("visit", None),
        P(),
        P(),
        P("visit", None, None),
        P("visit", None),
        P("visit", None, "tile"),
    )
    return jax.shard_map(
        body,
        mesh=mesh,
        in_specs=placed,
        out_specs=(P("tile", None), P("tile", None)),
        check_vma=False,
    )
```

```python
import jax
import jax.numpy as jnp
from jax import lax
from jax.experimental import pallas as pl
from jax.experimental.pallas import tpu as pltpu
from jax.sharding import PartitionSpec as P

MESH = pl.DeviceIdType.MESH
F32 = jnp.float32
BF16 = jnp.bfloat16
TAPS = 21
RIM = 10
BASES = 5
LANCZOS = 6
BLOCK = 32
SLAB = 128
PAD = 520
NV = 8
NT = 32
ROWS = NT * BLOCK
WIDTH = NT * SLAB
PAIRS = NT // 2
CHUNKS = 4
SPAN = WIDTH // CHUNKS
HALF = WIDTH // 2
FOLD = SPAN * RIM // 16


def split(x):
    high = x.astype(BF16)
    return high, (x - high.astype(F32)).astype(BF16)


def cols(j, n=SLAB):
    return pl.ds(pl.multiple_of(j * n, n), n)


def far_first(n):
    return sorted(range(n), key=lambda gap: -min(gap, n - gap))


def kernel(
    image_hbm, variance_hbm, mask_hbm, shift, coef_hbm, vert_hbm, horiz_hbm, colw_hbm, coloff_hbm, roww_hbm,
    final,
    mask, coef, vert, horiz, colw, coloff, roww,
    image, variance, folded, opened, h_send, h_recv,
    x_cat, v_mat, e_hi, e_lo, o_hi, o_lo, t_main_hi, t_main_lo, t_halo_hi, t_halo_lo,
    matched, factor, rw_mine, rw_quad, rw_all, s_iv, r_iv, s_cw, r_cw, ivf, cwf, wbi,
    nb_iv, nb_nu, c2_iv, c2_nu, total_iv, c3_iv, c3_nu,
    in_sem, halo_send, halo_recv, send_sem, recv_sem,
):
    v, t = lax.axis_index("visit"), lax.axis_index("tile")
    f_nu, f_iv = final.at[pl.ds(0, BLOCK)], final.at[pl.ds(BLOCK, BLOCK)]
    x, z = lax.div(t, 8), lax.rem(t, 8)
    y, core = lax.div(v, 2), lax.rem(v, 2)
    side = lax.div(t, NT // 2)
    to_self = (side == core) & (lax.rem(16 - 2 * z, 4) == y)

    get_image = pltpu.make_async_copy(image_hbm.at[0], image, in_sem.at[0])
    get_variance = pltpu.make_async_copy(variance_hbm.at[0], variance, in_sem.at[1])
    get_image.start()
    small = [
        pltpu.make_async_copy(source, target, in_sem.at[i + 2])
        for i, (source, target) in enumerate((
            (mask_hbm, mask), (roww_hbm, roww), (coef_hbm, coef), (vert_hbm, vert),
            (horiz_hbm, horiz), (colw_hbm, colw), (coloff_hbm, coloff)))
    ]
    for get in small:
        get.start()
    get_variance.start()

    barrier = pltpu.get_barrier_semaphore()

    def greet(v2, t2):
        pl.semaphore_signal(barrier, inc=1, device_id=(v2, t2), device_id_type=MESH)

    x_at = [8 * lax.rem(x + gap, 4) for gap in range(4)]
    z_at = [lax.rem(z + gap, 8) for gap in range(8)]
    y_at = [2 * lax.rem(y + gap, 4) for gap in range(4)]
    tiles = sorted(((dx, dz) for dx in range(4) for dz in range(8)), key=lambda gap: -min(gap[0], 4 - gap[0]) - min(gap[1], 8 - gap[1]))
    for dz in far_first(8)[:-1]:
        greet(v, 8 * x + z_at[dz])
    for dx in (2, 1, 3):
        greet(v, x_at[dx] + z)
    for step in (1, NT - 1):
        greet(v, lax.rem(t + step, NT))
    other = 1 - core
    for gap in (2, 1, 3):
        greet(y_at[gap] + core, t)
        greet(y_at[gap] + other, t)
    greet(y_at[0] + other, t)

    get_image.wait()

    def folds(row):
        return (
            (slice(row, row + 10), 0, slice(0, 10), 0, FOLD),
            (slice(row, row + 6), FOLD, slice(10, 16), 0, 384),
            (slice(row + 6, row + 10), FOLD, slice(10, 14), 384, 256),
            (slice(row + 6, row + 8), FOLD + 256, slice(14, 16), 384, 128),
            (slice(row + 8, row + 10), FOLD + 256, slice(14, 16), 512, 128),
        )

    def pack(g, c):
        for way, row in ((0, BLOCK - RIM), (1, 0)):
            for rows, start, to_rows, to_start, size in folds(row):
                at = pl.ds(pl.multiple_of(SPAN * g + start, SLAB), size)
                folded[to_rows, to_start:to_start + size] = image[rows, at]
            h_send[way, g] = folded[...].astype(BF16)
        return c

    lax.fori_loop(0, CHUNKS, pack, 0)
    pl.semaphore_wait(barrier, 7 + 3 + 2 + (NV - 1))

    def halo(way, g):
        return pltpu.make_async_remote_copy(
            src_ref=h_send.at[way, g], dst_ref=h_recv.at[way, g],
            send_sem=halo_send.at[way, g], recv_sem=halo_recv.at[way, g],
            device_id=(v, lax.rem(t + (1, NT - 1)[way], NT)), device_id_type=MESH)

    def start_halo(g, c):
        halo(0, g).start()
        halo(1, g).start()
        return c

    lax.fori_loop(0, CHUNKS, start_halo, 0)

    def fill_low(j, c):
        high = image[:, cols(j, 512)].astype(BF16)
        x_cat[16:48, cols(j, 512)] = high
        x_cat[112:144, cols(j, 512)] = high
        x_cat[64:96, cols(j, 512)] = (image[:, cols(j, 512)] - high.astype(F32)).astype(BF16)
        return c


    def send(source, target, at, v2, t2):
        pltpu.make_async_remote_copy(
            src_ref=source, dst_ref=target, send_sem=send_sem.at[at], recv_sem=recv_sem.at[at],
            device_id=(v2, t2), device_id_type=MESH).start()

    def arrived(ref, at):
        pltpu.make_async_copy(ref, ref, recv_sem.at[at]).wait()

    def left(ref, at):
        pltpu.make_async_copy(ref, ref, send_sem.at[at]).wait()

    for get in small:
        get.wait()
    rw_mine[...] = jnp.zeros_like(rw_mine)
    for q in range(4):
        for k in range(LANCZOS):
            rw_mine[k:k + 1, BLOCK * q:BLOCK * (q + 1)] = roww[k]
    lane = lax.broadcasted_iota(jnp.int32, (8, SLAB), 1)
    rw_mine[...] = jnp.where(lax.div(lane, BLOCK) == x, rw_mine[...], 0.0)
    for dx in (2, 1, 3):
        send(rw_mine, rw_quad.at[x], 6, v, x_at[dx] + z)
    rw_quad[x] = rw_mine[...]

    flags = jnp.broadcast_to(mask[...].astype(F32), (BLOCK, BLOCK))
    same = lax.broadcasted_iota(jnp.int32, (BLOCK, BLOCK), 0) == lax.broadcasted_iota(jnp.int32, (BLOCK, BLOCK), 1)
    usable = jnp.sum(jnp.where(same, flags, 0.0), axis=1, keepdims=True)
    get_variance.wait()

    def weigh(j, c):
        s_iv[j] = (usable / variance[:, cols(j)]).astype(BF16)
        return c

    lax.fori_loop(0, NT, weigh, 0)

    def send_iv(gaps):
        for dx, dz in gaps:
            t2 = x_at[dx] + z_at[dz]
            send(s_iv.at[t2], r_iv.at[t], 0, v, t2)

    send_iv([gap for gap in tiles[:-1] if gap[0] == 0])
    r_iv[t] = s_iv[t]
    lax.fori_loop(0, WIDTH // 512, fill_low, 0)

    r_at = lax.broadcasted_iota(jnp.int32, (BLOCK, 160), 0)
    q_at = lax.broadcasted_iota(jnp.int32, (BLOCK, 160), 1)
    q_row = jnp.where(q_at < 64, q_at - 16, jnp.where(q_at < 96, q_at - 64, q_at - 112))
    tap = q_row - r_at + RIM
    for b in range(BASES):
        value = jnp.zeros((BLOCK, 160), F32)
        for i in range(TAPS):
            value = jnp.where(tap == i, coef[0, b] * vert[b, i], value)
        high = value.astype(BF16).astype(F32)
        v_mat[BLOCK * b:BLOCK * (b + 1), :] = jnp.where(q_at < 96, high, value - high).astype(BF16)

    arrived(rw_quad.at[pl.ds(0, 3)], 6)
    send_iv([gap for gap in tiles if gap[0]])
    rw_all[z] = rw_quad[0] + rw_quad[1] + rw_quad[2] + rw_quad[3]
    for dz in far_first(8)[:-1]:
        send(rw_all.at[z], rw_all.at[z], 7, v, 8 * x + z_at[dz])

    n_at = lax.broadcasted_iota(jnp.int32, (16, 256), 1)
    k_at = lax.broadcasted_iota(jnp.int32, (16, 256), 0)

    def band(d):
        values = [jnp.zeros((16, 256), F32) for _ in range(BASES)]
        for i in range(TAPS):
            hit = d == i
            values = [jnp.where(hit, horiz[b, i], values[b]) for b in range(BASES)]
        return [split(value) for value in values]

    def build(c, carry):
        parts = band(16 * c + k_at - n_at + RIM)
        at = pl.ds(pl.multiple_of(16 * c, 16), 16)
        for b in range(BASES):
            t_main_hi[b, at, :], t_main_lo[b, at, :] = parts[b]
            t_halo_hi[b, at, :] = jnp.zeros((16, 256), BF16)
            t_halo_lo[b, at, :] = jnp.zeros((16, 256), BF16)
        return carry

    lax.fori_loop(0, 16, build, 0)
    for start, gap in ((112, -118), (128, 138)):
        parts = band(start + k_at - n_at + gap)
        for b in range(BASES):
            t_halo_hi[b, start:start + 16, :], t_halo_lo[b, start:start + 16, :] = parts[b]

    c_at = lax.broadcasted_iota(jnp.int32, (1, 512), 1)

    def weights(g, c):
        delta = coloff[0:1, cols(g, 512)] - (c_at + 512 * g)
        sums = [jnp.zeros((1, 512), F32) for _ in range(11)]
        for gap in range(-5, 1):
            hit = delta == gap
            for k in range(LANCZOS):
                sums[gap + k + 5] = sums[gap + k + 5] + jnp.where(hit, colw[k, :, cols(g, 512)], 0.0)
        for d in range(11):
            factor[d:d + 1, cols(g, 512)] = sums[d]
        return c

    lax.fori_loop(0, WIDTH // 512, weights, 0)

    for ref in (e_hi, e_lo):
        ref[:, PAIRS] = jnp.zeros((BASES, BLOCK, SLAB), BF16)
    for ref in (o_hi, o_lo):
        ref[:, 0] = jnp.zeros((BASES, BLOCK, SLAB), BF16)
    matched[:, 0:SLAB] = jnp.zeros((BLOCK, SLAB), F32)
    matched[:, SLAB + WIDTH:] = jnp.zeros((BLOCK, SLAB), F32)
    for ref in (ivf, cwf):
        ref[0:PAD, :] = jnp.zeros((PAD, SLAB), F32)
        ref[PAD + ROWS:, :] = jnp.zeros((8, SLAB), F32)

    def vertical(g):
        for way in range(2):
            halo(way, g).wait_recv()

        for way, row, present, first_row, second_row in ((0, 6, t > 0, 0, 96), (1, 0, t < NT - 1, 48, 144)):
            folded[...] = h_recv[way, g].astype(F32)
            opened[...] = jnp.zeros_like(opened)
            for rows, start, from_rows, from_start, size in folds(row):
                opened[rows, start:start + size] = folded[from_rows, from_start:from_start + size]
            near = jnp.where(present, opened[...], 0.0).astype(BF16)
            x_cat[first_row:first_row + 16, cols(g, SPAN)] = near
            x_cat[second_row:second_row + 16, cols(g, SPAN)] = near

        passed = jnp.dot(v_mat[...], x_cat[:, cols(g, SPAN)], preferred_element_type=F32)
        for i in range(4):
            j = 4 * g + i
            for b in range(BASES):
                high, low = split(passed[BLOCK * b:BLOCK * (b + 1), 256 * i:256 * (i + 1)])
                e_hi[b, j], o_hi[b, j + 1] = high[:, :SLAB], high[:, SLAB:]
                e_lo[b, j], o_lo[b, j + 1] = low[:, :SLAB], low[:, SLAB:]

    def horizontal(g):
        def part(ref, b, start):
            return ref[b, pl.ds(4 * g + start, 4)].reshape(4 * BLOCK, SLAB)

        total = jnp.zeros((4 * BLOCK, 256), F32)
        for b in range(BASES):
            main_hi = jnp.concatenate([part(e_hi, b, 0), part(o_hi, b, 1)], axis=1)
            main_lo = jnp.concatenate([part(e_lo, b, 0), part(o_lo, b, 1)], axis=1)
            halo_hi = jnp.concatenate([part(o_hi, b, 0), part(e_hi, b, 1)], axis=1)
            halo_lo = jnp.concatenate([part(o_lo, b, 0), part(e_lo, b, 1)], axis=1)
            for data, matrix in (
                (main_hi, t_main_hi), (main_lo, t_main_hi), (main_hi, t_main_lo),
                (halo_hi, t_halo_hi), (halo_lo, t_halo_hi), (halo_hi, t_halo_lo),
            ):
                total = total + jnp.dot(data, matrix[b], preferred_element_type=F32)
        for i in range(4):
            at = pl.ds(pl.multiple_of(SPAN * g + 256 * i + SLAB, SLAB), 256)
            matched[:, at] = total[BLOCK * i:BLOCK * (i + 1)]

    def interpolate(g):
        def step(i, c):
            j = 2 * g + i
            for r in range(2):
                window = matched[16 * r:16 * (r + 1), pl.ds(pl.multiple_of(512 * j, 512), 768)]
                total = jnp.zeros((16, 512), F32)
                for d in range(-5, 6):
                    moved = pltpu.roll(window, (-d) % 768, 1) if d else window
                    total = total + factor[d + 5:d + 6, cols(j, 512)] * moved[:, SLAB:SLAB + 512]
                total = total.astype(BF16)
                for q in range(4):
                    s_cw[4 * j + q, 16 * r:16 * (r + 1), :] = total[:, SLAB * q:SLAB * (q + 1)]
            return c

        lax.fori_loop(0, 2, step, 0)

    def send_cw(g):
        for dz in far_first(8)[:-1]:
            t2 = 8 * g + z_at[dz]
            send(s_cw.at[t2], r_cw.at[t], 1, v, t2)

        @pl.when(g != x)
        def _():
            send(s_cw.at[8 * g + z], r_cw.at[t], 1, v, 8 * g + z)

    def chunk(s, c):
        @pl.when(s < CHUNKS)
        def _():
            vertical(s)

        @pl.when((s >= 1) & (s < CHUNKS + 1))
        def _():
            horizontal(s - 1)

        @pl.when(s >= 2)
        def _():
            interpolate(s - 2)
            send_cw(s - 2)

        return c

    lax.fori_loop(0, CHUNKS + 2, chunk, 0)
    r_cw[t] = s_cw[t]

    def unpack(ref, target):
        def step(j, c):
            target[pl.ds(pl.multiple_of(PAD + 8 * BLOCK * j, 8), 8 * BLOCK), :] = ref[pl.ds(8 * j, 8)].reshape(8 * BLOCK, SLAB).astype(F32)
            return c

        lax.fori_loop(0, NT // 8, step, 0)

    def share(ref, x2, z2, plane):
        u2 = 2 * lax.rem(x2 + 24 - z2 - x - z, 4)
        ref[z2, pl.ds(u2, 2)] = plane.astype(BF16).reshape(2, 16, SLAB)

    def rows_of(x2, z2):
        return 8 * BLOCK * x2 + pl.multiple_of(BLOCK * z2, BLOCK)

    arrived(r_iv.at[pl.ds(0, NT - 1)], 0)
    arrived(rw_all.at[pl.ds(0, 7)], 7)
    unpack(r_iv, ivf)
    amount = shift[0]
    pick = lax.broadcasted_iota(jnp.int32, (16, LANCZOS * SLAB), 0)
    pick = lax.rem(pick, 8) == lax.div(lax.broadcasted_iota(jnp.int32, (16, LANCZOS * SLAB), 1), SLAB)
    pick = pick.astype(F32).astype(BF16)
    row_at = lax.broadcasted_iota(jnp.int32, (BLOCK, SLAB), 0)

    def spread(z2, c):
        whole = rw_all[z2]
        high = whole.astype(BF16).astype(F32)
        joined = jnp.concatenate([high, whole - high], axis=0).astype(BF16)
        wide = lax.dot_general(joined, pick, (((0,), (0,)), ((), ())), preferred_element_type=F32)
        for x2 in range(4):
            start = rows_of(x2, z2)
            sky = ivf[pl.ds(start + PAD - amount, BLOCK), :]
            share(nb_iv, x2, z2, sky)
            for k in range(LANCZOS):
                inside = row_at + (start + k - 2) < ROWS
                weight = wide[BLOCK * x2:BLOCK * (x2 + 1), SLAB * k:SLAB * (k + 1)]
                wbi[k, pl.ds(start, BLOCK), :] = jnp.where(inside, weight * sky, 0.0)
        return c

    lax.fori_loop(0, 8, spread, 0)

    first = 1 - lax.div(z, 4)

    def half(h):
        return pl.ds(4 * h, 4)

    def scatter(source, target, at, h):
        for gap in (2, 1, 3, 0):
            for seat in (core, other) if gap else (other,):
                v2 = y_at[gap] + seat
                send(source.at[half(h), v2], target.at[v, half(h)], at, v2, t)
        target[v, half(h)] = source[half(h), v]

    def deliver(source, target, at, h, own):
        rows, columns = pl.ds(pl.multiple_of(16 * core, 16), 16), cols(t)
        for turn in (2, 1, 3, 0) if own else (0, 1, 3, 2):
            z2 = 4 * h + lax.rem(z + turn, 4)
            t2 = 8 * lax.rem(y + z2 + x + z, 4) + z2
            for gap in (2, 1, 3):
                send(source.at[z2], target.at[rows, columns], at, y_at[gap] + side, t2)
            if turn or not own:
                send(source.at[z2], target.at[rows, columns], at, y_at[0] + side, t2)
        if not own:
            return
        me = (side == core) & (t2 == t)

        @pl.when(jnp.logical_not(me))
        def _():
            send(source.at[z], target.at[rows, columns], at, y_at[0] + side, t2)

        @pl.when(me)
        def _():
            pltpu.make_async_copy(source.at[z], target.at[rows, columns], recv_sem.at[at]).start()

    def swap(target, at):
        mine = target.at[:, cols(core, HALF)]
        send(mine, mine, at, v + 1 - 2 * core, t)

    def summed(ref, i):
        total = ref[0, i].astype(F32)
        for u in range(1, NV):
            total = total + ref[u, i].astype(F32)
        return total

    for h, at in ((first, 2), (1 - first, 10)):
        scatter(nb_iv, c2_iv, at, h)

    arrived(r_cw.at[pl.ds(0, NT - 1)], 1)
    unpack(r_cw, cwf)

    def warp(z2, c):
        for x2 in range(4):
            start = rows_of(x2, z2)
            total = jnp.zeros((BLOCK, SLAB), F32)
            for k in range(LANCZOS):
                total = total + wbi[k, pl.ds(start, BLOCK), :] * cwf[pl.ds(start + PAD + k - 2 - amount, BLOCK), :]
            share(nb_nu, x2, z2, total)
        return c

    for h, at in ((first, 3), (1 - first, 11)):
        lax.fori_loop(4 * h, 4 * h + 4, warp, 0)
        scatter(nb_nu, c2_nu, at, h)

    def add_iv(i, c):
        total = summed(c2_iv, i)
        total_iv[i] = total
        c3_iv[i] = total.astype(BF16)
        return c

    for h, at, own in ((first, 2, False), (1 - first, 10, True)):
        arrived(c2_iv.at[pl.ds(0, NV - 1), half(0)], at)
        lax.fori_loop(4 * h, 4 * h + 4, add_iv, 0)
        deliver(c3_iv, f_iv, 4, h, own)

    def add_nu(i, c):
        c3_nu[i] = (summed(c2_nu, i) / jnp.maximum(total_iv[i], 1.0)).astype(BF16)
        return c

    for h, at, own in ((first, 3, False), (1 - first, 11, True)):
        arrived(c2_nu.at[pl.ds(0, NV - 1), half(0)], at)
        lax.fori_loop(4 * h, 4 * h + 4, add_nu, 0)
        deliver(c3_nu, f_nu, 5, h, own)

    arrived(f_iv.at[:, pl.ds(0, HALF)], 4)
    swap(f_iv, 8)
    arrived(f_nu.at[:, pl.ds(0, HALF)], 5)
    swap(f_nu, 9)

    def halo_left(g, c):
        halo(0, g).wait_send()
        halo(1, g).wait_send()
        return c

    lax.fori_loop(0, CHUNKS, halo_left, 0)
    left(rw_quad.at[pl.ds(0, 3)], 6)
    left(rw_all.at[pl.ds(0, 7)], 7)
    left(s_iv.at[pl.ds(0, NT - 1)], 0)
    left(s_cw.at[pl.ds(0, NT - 1)], 1)
    for target, at in ((c2_iv, 2), (c2_iv, 10), (c2_nu, 3), (c2_nu, 11)):
        left(target.at[pl.ds(0, NV - 1), half(0)], at)
    for c3, at in ((c3_iv, 4), (c3_nu, 5)):
        @pl.when(to_self)
        def _():
            left(c3.at[pl.ds(0, NT - 1)], at)

        @pl.when(jnp.logical_not(to_self))
        def _():
            left(c3, at)

    for target, at in ((f_iv, 8), (f_nu, 9)):
        left(target.at[:, pl.ds(0, HALF)], at)
        arrived(target.at[:, pl.ds(0, HALF)], at)


def solution(mesh):
    def body(image, variance, mask, shift, coef, vert, horiz, colw, coloff, roww):
        vmem = pl.BlockSpec(memory_space=pltpu.VMEM)
        smem = pl.BlockSpec(memory_space=pltpu.SMEM)
        hbm = pl.BlockSpec(memory_space=pltpu.HBM)

        def plane(*shape, dtype=BF16):
            return pltpu.VMEM(shape, dtype)

        def keep(array):
            return pltpu.with_memory_space_constraint(array, pltpu.HBM)

        both = pl.pallas_call(
            kernel,
            out_shape=jax.ShapeDtypeStruct((2 * BLOCK, WIDTH), BF16),
            in_specs=[hbm, hbm, hbm, smem, *[hbm] * 6],
            out_specs=vmem,
            scratch_shapes=[
                plane(1, BLOCK, dtype=jnp.int32),
                pltpu.SMEM((1, BASES), F32),
                pltpu.SMEM((BASES, TAPS), F32),
                pltpu.SMEM((BASES, TAPS), F32),
                plane(LANCZOS, 1, WIDTH, dtype=F32),
                plane(1, WIDTH, dtype=jnp.int32),
                plane(LANCZOS, 1, BLOCK, dtype=F32),
                *[plane(BLOCK, WIDTH, dtype=F32)] * 2,
                plane(16, FOLD, dtype=F32),
                plane(16, SPAN, dtype=F32),
                *[plane(2, CHUNKS, 16, FOLD)] * 2,
                plane(160, WIDTH),
                plane(160, 160),
                *[plane(BASES, PAIRS + 1, BLOCK, SLAB)] * 4,
                *[plane(BASES, 256, 256)] * 4,
                plane(BLOCK, WIDTH + 2 * SLAB, dtype=F32),
                plane(16, WIDTH, dtype=F32),
                plane(8, SLAB, dtype=F32),
                plane(4, 8, SLAB, dtype=F32),
                plane(8, 8, SLAB, dtype=F32),
                *[plane(NT, BLOCK, SLAB)] * 4,
                *[plane(PAD + ROWS + 8, SLAB, dtype=F32)] * 2,
                plane(LANCZOS, ROWS, SLAB, dtype=F32),
                *[plane(8, NV, 16, SLAB)] * 2,
                *[plane(NV, 8, 16, SLAB)] * 2,
                plane(8, 16, SLAB, dtype=F32),
                *[plane(NT, 16, SLAB)] * 2,
                pltpu.SemaphoreType.DMA((9,)),
                pltpu.SemaphoreType.DMA((2, CHUNKS)),
                pltpu.SemaphoreType.DMA((2, CHUNKS)),
                pltpu.SemaphoreType.DMA((12,)),
                pltpu.SemaphoreType.DMA((12,)),
            ],
            compiler_params=pltpu.CompilerParams(
                collective_id=0, has_side_effects=True, vmem_limit_bytes=48 * 2**20
            ),
        )(keep(image), keep(variance), keep(mask), shift, keep(coef), keep(vert), keep(horiz),
          keep(jnp.transpose(colw, (1, 0, 2))), keep(coloff), keep(jnp.transpose(roww, (1, 0, 2))))
        both = both.astype(F32)
        return both[:BLOCK], both[BLOCK:]

    placed = (
        P("visit", "tile", None),
        P("visit", "tile", None),
        P("visit", "tile"),
        P("visit"),
        P("visit", None),
        P(),
        P(),
        P("visit", None, None),
        P("visit", None),
        P("visit", None, "tile"),
    )
    return jax.shard_map(
        body,
        mesh=mesh,
        in_specs=placed,
        out_specs=(P("tile", None), P("tile", None)),
        check_vma=False,
    )
```

```python
import jax
import jax.numpy as jnp
from jax import lax
from jax.experimental import pallas as pl
from jax.experimental.pallas import tpu as pltpu
from jax.sharding import PartitionSpec as P

MESH = pl.DeviceIdType.MESH
F32 = jnp.float32
BF16 = jnp.bfloat16
TAPS = 21
RIM = 10
BASES = 5
LANCZOS = 6
BLOCK = 32
SLAB = 128
PAD = 520
PART = 2
NV = 8
NT = 32
ROWS = NT * BLOCK
WIDTH = NT * SLAB
PAIRS = NT // 2
CHUNKS = 4
SPAN = WIDTH // CHUNKS
HALF = WIDTH // 2
FOLD = SPAN * RIM // 16


def split(x):
    high = x.astype(BF16)
    return high, (x - high.astype(F32)).astype(BF16)


def cols(j, n=SLAB):
    return pl.ds(pl.multiple_of(j * n, n), n)


def far_first(n):
    return sorted(range(n), key=lambda gap: -min(gap, n - gap))


def kernel(
    image_hbm, variance_hbm, mask_hbm, shift, coef_hbm, vert_hbm, horiz_hbm, colw_hbm, coloff_hbm, roww_hbm,
    final,
    mask, coef, vert, horiz, colw, coloff, roww,
    image, variance, folded, opened, h_send, h_recv,
    x_cat, v_mat, e_hi, e_lo, o_hi, o_lo, t_main_hi, t_main_lo, t_halo_hi, t_halo_lo,
    matched, factor, rw_mine, rw_quad, rw_all, s_iv, r_iv, s_cw, r_cw, ivf, cwf, wbi,
    nb_iv, nb_nu, c2_iv, c2_nu, total_iv, c3_iv, c3_nu,
    in_sem, halo_send, halo_recv, send_sem, recv_sem,
):
    v, t = lax.axis_index("visit"), lax.axis_index("tile")
    f_nu, f_iv = final.at[pl.ds(0, BLOCK)], final.at[pl.ds(BLOCK, BLOCK)]
    x, z = lax.div(t, 8), lax.rem(t, 8)
    y, core = lax.div(v, 2), lax.rem(v, 2)
    side = lax.div(t, NT // 2)
    to_self = (side == core) & (lax.rem(16 - 2 * z, 4) == y)

    get_image = pltpu.make_async_copy(image_hbm.at[0], image, in_sem.at[0])
    get_variance = pltpu.make_async_copy(variance_hbm.at[0], variance, in_sem.at[1])
    get_image.start()
    small = [
        pltpu.make_async_copy(source, target, in_sem.at[i + 2])
        for i, (source, target) in enumerate((
            (mask_hbm, mask), (roww_hbm, roww), (coef_hbm, coef), (vert_hbm, vert),
            (horiz_hbm, horiz), (colw_hbm, colw), (coloff_hbm, coloff)))
    ]
    for get in small:
        get.start()
    get_variance.start()

    barrier = pltpu.get_barrier_semaphore()

    def greet(v2, t2):
        pl.semaphore_signal(barrier, inc=1, device_id=(v2, t2), device_id_type=MESH)

    x_at = [8 * lax.rem(x + gap, 4) for gap in range(4)]
    z_at = [lax.rem(z + gap, 8) for gap in range(8)]
    y_at = [2 * lax.rem(y + gap, 4) for gap in range(4)]
    tiles = sorted(((dx, dz) for dx in range(4) for dz in range(8)), key=lambda gap: -min(gap[0], 4 - gap[0]) - min(gap[1], 8 - gap[1]))
    for dz in far_first(8)[:-1]:
        greet(v, 8 * x + z_at[dz])
    for dx in (2, 1, 3):
        greet(v, x_at[dx] + z)
    for step in (1, NT - 1):
        greet(v, lax.rem(t + step, NT))
    other = 1 - core
    for gap in (2, 1, 3):
        greet(y_at[gap] + core, t)
        greet(y_at[gap] + other, t)
    greet(y_at[0] + other, t)

    get_image.wait()

    def folds(row):
        return (
            (slice(row, row + 10), 0, slice(0, 10), 0, FOLD),
            (slice(row, row + 6), FOLD, slice(10, 16), 0, 384),
            (slice(row + 6, row + 10), FOLD, slice(10, 14), 384, 256),
            (slice(row + 6, row + 8), FOLD + 256, slice(14, 16), 384, 128),
            (slice(row + 8, row + 10), FOLD + 256, slice(14, 16), 512, 128),
        )

    def pack(g, c):
        for way, row in ((0, BLOCK - RIM), (1, 0)):
            for rows, start, to_rows, to_start, size in folds(row):
                at = pl.ds(pl.multiple_of(SPAN * g + start, SLAB), size)
                folded[to_rows, to_start:to_start + size] = image[rows, at]
            h_send[way, g] = folded[...].astype(BF16)
        return c

    lax.fori_loop(0, CHUNKS, pack, 0)
    pl.semaphore_wait(barrier, 7 + 3 + 2 + (NV - 1))

    def halo(way, g):
        return pltpu.make_async_remote_copy(
            src_ref=h_send.at[way, g], dst_ref=h_recv.at[way, g],
            send_sem=halo_send.at[way, g], recv_sem=halo_recv.at[way, g],
            device_id=(v, lax.rem(t + (1, NT - 1)[way], NT)), device_id_type=MESH)

    def start_halo(g, c):
        halo(0, g).start()
        halo(1, g).start()
        return c

    lax.fori_loop(0, CHUNKS, start_halo, 0)

    def fill_low(j, c):
        high = image[:, cols(j, 512)].astype(BF16)
        x_cat[16:48, cols(j, 512)] = high
        x_cat[112:144, cols(j, 512)] = high
        x_cat[64:96, cols(j, 512)] = (image[:, cols(j, 512)] - high.astype(F32)).astype(BF16)
        return c


    def send(source, target, at, v2, t2):
        pltpu.make_async_remote_copy(
            src_ref=source, dst_ref=target, send_sem=send_sem.at[at], recv_sem=recv_sem.at[at],
            device_id=(v2, t2), device_id_type=MESH).start()

    def arrived(ref, at):
        pltpu.make_async_copy(ref, ref, recv_sem.at[at]).wait()

    def left(ref, at):
        pltpu.make_async_copy(ref, ref, send_sem.at[at]).wait()

    for get in small:
        get.wait()
    rw_mine[...] = jnp.zeros_like(rw_mine)
    for q in range(4):
        for k in range(LANCZOS):
            rw_mine[k:k + 1, BLOCK * q:BLOCK * (q + 1)] = roww[k]
    lane = lax.broadcasted_iota(jnp.int32, (8, SLAB), 1)
    rw_mine[...] = jnp.where(lax.div(lane, BLOCK) == x, rw_mine[...], 0.0)
    for dx in (2, 1, 3):
        send(rw_mine, rw_quad.at[x], 6, v, x_at[dx] + z)
    rw_quad[x] = rw_mine[...]

    flags = jnp.broadcast_to(mask[...].astype(F32), (BLOCK, BLOCK))
    same = lax.broadcasted_iota(jnp.int32, (BLOCK, BLOCK), 0) == lax.broadcasted_iota(jnp.int32, (BLOCK, BLOCK), 1)
    usable = jnp.sum(jnp.where(same, flags, 0.0), axis=1, keepdims=True)
    get_variance.wait()

    def weigh(j, c):
        s_iv[j] = (usable / variance[:, cols(j)]).astype(BF16)
        return c

    lax.fori_loop(0, NT, weigh, 0)

    def send_iv(gaps):
        for dx, dz in gaps:
            t2 = x_at[dx] + z_at[dz]
            send(s_iv.at[t2], r_iv.at[t], 0, v, t2)

    send_iv([gap for gap in tiles[:-1] if gap[0] == 0])
    r_iv[t] = s_iv[t]
    lax.fori_loop(0, WIDTH // 512, fill_low, 0)

    r_at = lax.broadcasted_iota(jnp.int32, (BLOCK, 160), 0)
    q_at = lax.broadcasted_iota(jnp.int32, (BLOCK, 160), 1)
    q_row = jnp.where(q_at < 64, q_at - 16, jnp.where(q_at < 96, q_at - 64, q_at - 112))
    tap = q_row - r_at + RIM
    for b in range(BASES):
        value = jnp.zeros((BLOCK, 160), F32)
        for i in range(TAPS):
            value = jnp.where(tap == i, coef[0, b] * vert[b, i], value)
        high = value.astype(BF16).astype(F32)
        v_mat[BLOCK * b:BLOCK * (b + 1), :] = jnp.where(q_at < 96, high, value - high).astype(BF16)

    arrived(rw_quad.at[pl.ds(0, 3)], 6)
    send_iv([gap for gap in tiles if gap[0]])
    rw_all[z] = rw_quad[0] + rw_quad[1] + rw_quad[2] + rw_quad[3]
    for dz in far_first(8)[:-1]:
        send(rw_all.at[z], rw_all.at[z], 7, v, 8 * x + z_at[dz])

    n_at = lax.broadcasted_iota(jnp.int32, (16, 256), 1)
    k_at = lax.broadcasted_iota(jnp.int32, (16, 256), 0)

    def band(d):
        values = [jnp.zeros((16, 256), F32) for _ in range(BASES)]
        for i in range(TAPS):
            hit = d == i
            values = [jnp.where(hit, horiz[b, i], values[b]) for b in range(BASES)]
        return [split(value) for value in values]

    def build(c, carry):
        parts = band(16 * c + k_at - n_at + RIM)
        at = pl.ds(pl.multiple_of(16 * c, 16), 16)
        for b in range(BASES):
            t_main_hi[b, at, :], t_main_lo[b, at, :] = parts[b]
            t_halo_hi[b, at, :] = jnp.zeros((16, 256), BF16)
            t_halo_lo[b, at, :] = jnp.zeros((16, 256), BF16)
        return carry

    lax.fori_loop(0, 16, build, 0)
    for start, gap in ((112, -118), (128, 138)):
        parts = band(start + k_at - n_at + gap)
        for b in range(BASES):
            t_halo_hi[b, start:start + 16, :], t_halo_lo[b, start:start + 16, :] = parts[b]

    c_at = lax.broadcasted_iota(jnp.int32, (1, 512), 1)

    def weights(g, c):
        delta = coloff[0:1, cols(g, 512)] - (c_at + 512 * g)
        sums = [jnp.zeros((1, 512), F32) for _ in range(11)]
        for gap in range(-5, 1):
            hit = delta == gap
            for k in range(LANCZOS):
                sums[gap + k + 5] = sums[gap + k + 5] + jnp.where(hit, colw[k, :, cols(g, 512)], 0.0)
        for d in range(11):
            factor[d:d + 1, cols(g, 512)] = sums[d]
        return c

    lax.fori_loop(0, WIDTH // 512, weights, 0)

    for ref in (e_hi, e_lo):
        ref[:, PAIRS] = jnp.zeros((BASES, BLOCK, SLAB), BF16)
    for ref in (o_hi, o_lo):
        ref[:, 0] = jnp.zeros((BASES, BLOCK, SLAB), BF16)
    matched[:, 0:SLAB] = jnp.zeros((BLOCK, SLAB), F32)
    matched[:, SLAB + WIDTH:] = jnp.zeros((BLOCK, SLAB), F32)
    for ref in (ivf, cwf):
        ref[0:PAD, :] = jnp.zeros((PAD, SLAB), F32)
        ref[PAD + ROWS:, :] = jnp.zeros((8, SLAB), F32)

    def vertical(g):
        for way in range(2):
            halo(way, g).wait_recv()

        for way, row, present, first_row, second_row in ((0, 6, t > 0, 0, 96), (1, 0, t < NT - 1, 48, 144)):
            folded[...] = h_recv[way, g].astype(F32)
            opened[...] = jnp.zeros_like(opened)
            for rows, start, from_rows, from_start, size in folds(row):
                opened[rows, start:start + size] = folded[from_rows, from_start:from_start + size]
            near = jnp.where(present, opened[...], 0.0).astype(BF16)
            x_cat[first_row:first_row + 16, cols(g, SPAN)] = near
            x_cat[second_row:second_row + 16, cols(g, SPAN)] = near

        passed = jnp.dot(v_mat[...], x_cat[:, cols(g, SPAN)], preferred_element_type=F32)
        for i in range(4):
            j = 4 * g + i
            for b in range(BASES):
                high, low = split(passed[BLOCK * b:BLOCK * (b + 1), 256 * i:256 * (i + 1)])
                e_hi[b, j], o_hi[b, j + 1] = high[:, :SLAB], high[:, SLAB:]
                e_lo[b, j], o_lo[b, j + 1] = low[:, :SLAB], low[:, SLAB:]

    def horizontal(g):
        def part(ref, b, start):
            return ref[b, pl.ds(4 * g + start, 4)].reshape(4 * BLOCK, SLAB)

        total = jnp.zeros((4 * BLOCK, 256), F32)
        for b in range(BASES):
            main_hi = jnp.concatenate([part(e_hi, b, 0), part(o_hi, b, 1)], axis=1)
            main_lo = jnp.concatenate([part(e_lo, b, 0), part(o_lo, b, 1)], axis=1)
            halo_hi = jnp.concatenate([part(o_hi, b, 0), part(e_hi, b, 1)], axis=1)
            halo_lo = jnp.concatenate([part(o_lo, b, 0), part(e_lo, b, 1)], axis=1)
            for data, matrix in (
                (main_hi, t_main_hi), (main_lo, t_main_hi), (main_hi, t_main_lo),
                (halo_hi, t_halo_hi), (halo_lo, t_halo_hi), (halo_hi, t_halo_lo),
            ):
                total = total + jnp.dot(data, matrix[b], preferred_element_type=F32)
        for i in range(4):
            at = pl.ds(pl.multiple_of(SPAN * g + 256 * i + SLAB, SLAB), 256)
            matched[:, at] = total[BLOCK * i:BLOCK * (i + 1)]

    def interpolate(g):
        def step(i, c):
            j = 2 * g + i
            for r in range(2):
                window = matched[16 * r:16 * (r + 1), pl.ds(pl.multiple_of(512 * j, 512), 768)]
                total = jnp.zeros((16, 512), F32)
                for d in range(-5, 6):
                    moved = pltpu.roll(window, (-d) % 768, 1) if d else window
                    total = total + factor[d + 5:d + 6, cols(j, 512)] * moved[:, SLAB:SLAB + 512]
                total = total.astype(BF16)
                for q in range(4):
                    s_cw[4 * j + q, 16 * r:16 * (r + 1), :] = total[:, SLAB * q:SLAB * (q + 1)]
            return c

        lax.fori_loop(0, 2, step, 0)

    def send_cw(g):
        for dz in far_first(8)[:-1]:
            t2 = 8 * g + z_at[dz]
            send(s_cw.at[t2], r_cw.at[t], 1, v, t2)

        @pl.when(g != x)
        def _():
            send(s_cw.at[8 * g + z], r_cw.at[t], 1, v, 8 * g + z)

    def chunk(s, c):
        @pl.when(s < CHUNKS)
        def _():
            vertical(s)

        @pl.when((s >= 1) & (s < CHUNKS + 1))
        def _():
            horizontal(s - 1)

        @pl.when(s >= 2)
        def _():
            interpolate(s - 2)
            send_cw(s - 2)

        return c

    lax.fori_loop(0, CHUNKS + 2, chunk, 0)
    r_cw[t] = s_cw[t]

    def unpack(ref, target):
        def step(j, c):
            target[pl.ds(pl.multiple_of(PAD + 8 * BLOCK * j, 8), 8 * BLOCK), :] = ref[pl.ds(8 * j, 8)].reshape(8 * BLOCK, SLAB).astype(F32)
            return c

        lax.fori_loop(0, NT // 8, step, 0)

    def share(ref, x2, z2, plane):
        u2 = 2 * lax.rem(x2 + 24 - z2 - x - z, 4)
        ref[z2, pl.ds(u2, 2)] = plane.astype(BF16).reshape(2, 16, SLAB)

    def rows_of(x2, z2):
        return 8 * BLOCK * x2 + pl.multiple_of(BLOCK * z2, BLOCK)

    arrived(r_iv.at[pl.ds(0, NT - 1)], 0)
    arrived(rw_all.at[pl.ds(0, 7)], 7)
    unpack(r_iv, ivf)
    amount = shift[0]
    pick = lax.broadcasted_iota(jnp.int32, (16, LANCZOS * SLAB), 0)
    pick = lax.rem(pick, 8) == lax.div(lax.broadcasted_iota(jnp.int32, (16, LANCZOS * SLAB), 1), SLAB)
    pick = pick.astype(F32).astype(BF16)
    row_at = lax.broadcasted_iota(jnp.int32, (BLOCK, SLAB), 0)

    def spread(z2, c):
        whole = rw_all[z2]
        high = whole.astype(BF16).astype(F32)
        joined = jnp.concatenate([high, whole - high], axis=0).astype(BF16)
        wide = lax.dot_general(joined, pick, (((0,), (0,)), ((), ())), preferred_element_type=F32)
        for x2 in range(4):
            start = rows_of(x2, z2)
            sky = ivf[pl.ds(start + PAD - amount, BLOCK), :]
            share(nb_iv, x2, z2, sky)
            for k in range(LANCZOS):
                inside = row_at + (start + k - 2) < ROWS
                weight = wide[BLOCK * x2:BLOCK * (x2 + 1), SLAB * k:SLAB * (k + 1)]
                wbi[k, pl.ds(start, BLOCK), :] = jnp.where(inside, weight * sky, 0.0)
        return c

    lax.fori_loop(0, 8, spread, 0)

    parts = [(lax.rem(lax.div(z, PART) + gap, 8 // PART), i, gap == 0) for i, gap in enumerate(far_first(8 // PART))]

    def part(h):
        return pl.ds(PART * h, PART)

    def scatter(source, target, at, h):
        for gap in (2, 1, 3, 0):
            for seat in (core, other) if gap else (other,):
                v2 = y_at[gap] + seat
                send(source.at[part(h), v2], target.at[v, part(h)], at, v2, t)
        target[v, part(h)] = source[part(h), v]

    def deliver(source, target, at, h, own):
        rows, columns = pl.ds(pl.multiple_of(16 * core, 16), 16), cols(t)
        for turn in range(PART - 1, -1, -1):
            z2 = PART * h + lax.rem(z + turn, PART)
            t2 = 8 * lax.rem(y + z2 + x + z, 4) + z2
            for gap in (2, 1, 3):
                send(source.at[z2], target.at[rows, columns], at, y_at[gap] + side, t2)
            if turn or not own:
                send(source.at[z2], target.at[rows, columns], at, y_at[0] + side, t2)
        if not own:
            return
        me = (side == core) & (t2 == t)

        @pl.when(jnp.logical_not(me))
        def _():
            send(source.at[z], target.at[rows, columns], at, y_at[0] + side, t2)

        @pl.when(me)
        def _():
            pltpu.make_async_copy(source.at[z], target.at[rows, columns], recv_sem.at[at]).start()

    def swap(target, at):
        mine = target.at[:, cols(core, HALF)]
        send(mine, mine, at, v + 1 - 2 * core, t)

    def summed(ref, i):
        total = ref[0, i].astype(F32)
        for u in range(1, NV):
            total = total + ref[u, i].astype(F32)
        return total

    for h, i, own in parts:
        scatter(nb_iv, c2_iv, 10 + i, h)

    arrived(r_cw.at[pl.ds(0, NT - 1)], 1)
    unpack(r_cw, cwf)

    def warp(z2, c):
        for x2 in range(4):
            start = rows_of(x2, z2)
            total = jnp.zeros((BLOCK, SLAB), F32)
            for k in range(LANCZOS):
                total = total + wbi[k, pl.ds(start, BLOCK), :] * cwf[pl.ds(start + PAD + k - 2 - amount, BLOCK), :]
            share(nb_nu, x2, z2, total)
        return c

    for h, i, own in parts:
        lax.fori_loop(PART * h, PART * h + PART, warp, 0)
        scatter(nb_nu, c2_nu, 18 + i, h)

    def add_iv(i, c):
        total = summed(c2_iv, i)
        total_iv[i] = total
        c3_iv[i] = total.astype(BF16)
        return c

    for h, i, own in parts:
        arrived(c2_iv.at[pl.ds(0, NV - 1), part(0)], 10 + i)
        lax.fori_loop(PART * h, PART * h + PART, add_iv, 0)
        deliver(c3_iv, f_iv, 4, h, own)

    def add_nu(i, c):
        c3_nu[i] = (summed(c2_nu, i) / jnp.maximum(total_iv[i], 1.0)).astype(BF16)
        return c

    for h, i, own in parts:
        arrived(c2_nu.at[pl.ds(0, NV - 1), part(0)], 18 + i)
        lax.fori_loop(PART * h, PART * h + PART, add_nu, 0)
        deliver(c3_nu, f_nu, 5, h, own)

    arrived(f_iv.at[:, pl.ds(0, HALF)], 4)
    swap(f_iv, 8)
    arrived(f_nu.at[:, pl.ds(0, HALF)], 5)
    swap(f_nu, 9)

    def halo_left(g, c):
        halo(0, g).wait_send()
        halo(1, g).wait_send()
        return c

    lax.fori_loop(0, CHUNKS, halo_left, 0)
    left(rw_quad.at[pl.ds(0, 3)], 6)
    left(rw_all.at[pl.ds(0, 7)], 7)
    left(s_iv.at[pl.ds(0, NT - 1)], 0)
    left(s_cw.at[pl.ds(0, NT - 1)], 1)
    for h, i, own in parts:
        left(c2_iv.at[pl.ds(0, NV - 1), part(0)], 10 + i)
        left(c2_nu.at[pl.ds(0, NV - 1), part(0)], 18 + i)
    for c3, at in ((c3_iv, 4), (c3_nu, 5)):
        @pl.when(to_self)
        def _():
            left(c3.at[pl.ds(0, NT - 1)], at)

        @pl.when(jnp.logical_not(to_self))
        def _():
            left(c3, at)

    for target, at in ((f_iv, 8), (f_nu, 9)):
        left(target.at[:, pl.ds(0, HALF)], at)
        arrived(target.at[:, pl.ds(0, HALF)], at)


def solution(mesh):
    def body(image, variance, mask, shift, coef, vert, horiz, colw, coloff, roww):
        vmem = pl.BlockSpec(memory_space=pltpu.VMEM)
        smem = pl.BlockSpec(memory_space=pltpu.SMEM)
        hbm = pl.BlockSpec(memory_space=pltpu.HBM)

        def plane(*shape, dtype=BF16):
            return pltpu.VMEM(shape, dtype)

        def keep(array):
            return pltpu.with_memory_space_constraint(array, pltpu.HBM)

        both = pl.pallas_call(
            kernel,
            out_shape=jax.ShapeDtypeStruct((2 * BLOCK, WIDTH), BF16),
            in_specs=[hbm, hbm, hbm, smem, *[hbm] * 6],
            out_specs=vmem,
            scratch_shapes=[
                plane(1, BLOCK, dtype=jnp.int32),
                pltpu.SMEM((1, BASES), F32),
                pltpu.SMEM((BASES, TAPS), F32),
                pltpu.SMEM((BASES, TAPS), F32),
                plane(LANCZOS, 1, WIDTH, dtype=F32),
                plane(1, WIDTH, dtype=jnp.int32),
                plane(LANCZOS, 1, BLOCK, dtype=F32),
                *[plane(BLOCK, WIDTH, dtype=F32)] * 2,
                plane(16, FOLD, dtype=F32),
                plane(16, SPAN, dtype=F32),
                *[plane(2, CHUNKS, 16, FOLD)] * 2,
                plane(160, WIDTH),
                plane(160, 160),
                *[plane(BASES, PAIRS + 1, BLOCK, SLAB)] * 4,
                *[plane(BASES, 256, 256)] * 4,
                plane(BLOCK, WIDTH + 2 * SLAB, dtype=F32),
                plane(16, WIDTH, dtype=F32),
                plane(8, SLAB, dtype=F32),
                plane(4, 8, SLAB, dtype=F32),
                plane(8, 8, SLAB, dtype=F32),
                *[plane(NT, BLOCK, SLAB)] * 4,
                *[plane(PAD + ROWS + 8, SLAB, dtype=F32)] * 2,
                plane(LANCZOS, ROWS, SLAB, dtype=F32),
                *[plane(8, NV, 16, SLAB)] * 2,
                *[plane(NV, 8, 16, SLAB)] * 2,
                plane(8, 16, SLAB, dtype=F32),
                *[plane(NT, 16, SLAB)] * 2,
                pltpu.SemaphoreType.DMA((9,)),
                pltpu.SemaphoreType.DMA((2, CHUNKS)),
                pltpu.SemaphoreType.DMA((2, CHUNKS)),
                pltpu.SemaphoreType.DMA((26,)),
                pltpu.SemaphoreType.DMA((26,)),
            ],
            compiler_params=pltpu.CompilerParams(
                collective_id=0, has_side_effects=True, vmem_limit_bytes=48 * 2**20
            ),
        )(keep(image), keep(variance), keep(mask), shift, keep(coef), keep(vert), keep(horiz),
          keep(jnp.transpose(colw, (1, 0, 2))), keep(coloff), keep(jnp.transpose(roww, (1, 0, 2))))
        both = both.astype(F32)
        return both[:BLOCK], both[BLOCK:]

    placed = (
        P("visit", "tile", None),
        P("visit", "tile", None),
        P("visit", "tile"),
        P("visit"),
        P("visit", None),
        P(),
        P(),
        P("visit", None, None),
        P("visit", None),
        P("visit", None, "tile"),
    )
    return jax.shard_map(
        body,
        mesh=mesh,
        in_specs=placed,
        out_specs=(P("tile", None), P("tile", None)),
        check_vma=False,
    )
```
